128 devices in a mesh: lon: 16 (over y_hi, z, core), lat: 8 (over x, y_lo).
Axes of the slice: x: 4, y: 4 (y_hi: 2, y_lo: 2; y = y_hi * 2 + y_lo), z: 4, core: 2. Of those that a mesh axis runs over, the one named last changes fastest.
Arguments:
- state: bfloat16 [192, 768, 512], P('lat', 'lon'), may hold values from -6 to 6
- attention_in: bfloat16 [2, 512, 1536], replicated, may hold values from -10 to 10
- attention_out: bfloat16 [2, 512, 512], replicated, may hold values from -0.25 to 0.25
- expand_weight: bfloat16 [2, 512, 2048], replicated, may hold values from -0.25 to 0.25
- depth_kernel: bfloat16 [2, 7, 7, 2048], replicated, may hold values from -0.875 to 0.875
- shrink_weight: bfloat16 [2, 2048, 512], replicated, may hold values from -0.125 to 0.125
- norm_attention: float32 [2, 512], replicated, may hold values from 0.1 to 1.9
- norm_feedforward: float32 [2, 512], replicated, may hold values from 0.1 to 1.9
Outputs:
- advanced_state: bfloat16 [192, 768, 512], P('lat', 'lon')
The draws below stay inside these ranges and needn't reach their ends.
All inputs are finite; a program needn't handle non-finite values.
Results may differ from the reference program's by a relative error of at most 0.009.
Values may be sent and summed in bfloat16 or wider, within the bound.
No kernel may reach another device: no remote copies, remote signals or barrier semaphores. Data moves between devices by JAX's collectives and lax.ppermute only.
A program may use at most 128 MiB of HBM per device.

```python
import math
import jax
import jax.numpy as jnp
from jax import lax

D = 512
HEADS = 8
HEAD_DIM = 64
FF = 2048
RADIUS = 6
CONV_RADIUS = 3
LAYERS = 2
KERNEL = 7
NLAT = 192
NLON = 768


def draw_state(key, part):
    own_key = jax.random.fold_in(key, 71)
    first = jax.random.fold_in(own_key, 0)
    extent = (NLAT, NLON, D)
    base = jax.random.normal(first, extent, jnp.float32)
    return jnp.clip(base, -6.0, 6.0).astype(jnp.bfloat16)


def draw_attention_in(key, part):
    own_key = jax.random.fold_in(key, 72)
    first = jax.random.fold_in(own_key, 0)
    base = jnp.clip(jax.random.normal(first, (LAYERS, D, 3 * D), jnp.float32), -5.0, 5.0) * D ** (-0.5)
    return base.astype(jnp.bfloat16)


def noise(rng, shape, width, limit, held_as=jnp.bfloat16):
    return jnp.clip(width * jax.random.normal(rng, shape, jnp.float32), -limit, limit).astype(held_as)


def setup_inputs(seed: int = 0) -> dict:
    seeds = jax.random.split(jax.random.key(seed), 9)
    return {
        "state": draw_state(jax.random.fold_in(seeds[8], 71), 0),
        "attention_in": draw_attention_in(jax.random.fold_in(seeds[8], 71), 0),
        "attention_out": noise(seeds[2], (LAYERS, D, D), D ** -0.5, 0.25),
        "expand_weight": noise(seeds[3], (LAYERS, D, FF), D ** -0.5, 0.25),
        "depth_kernel": noise(seeds[4], (LAYERS, KERNEL, KERNEL, FF), (KERNEL * KERNEL) ** -0.5, 0.875),
        "shrink_weight": noise(seeds[5], (LAYERS, FF, D), FF ** -0.5, 0.125),
        "norm_attention": jnp.clip(1.0 + 0.18 * jax.random.normal(seeds[6], (LAYERS, D), jnp.float32), 0.1, 1.9),
        "norm_feedforward": jnp.clip(1.0 + 0.18 * jax.random.normal(seeds[7], (LAYERS, D), jnp.float32), 0.1, 1.9),
    }


def normalize(stream, gain):
    average = lax.optimization_barrier(jnp.mean(stream, axis=-1, keepdims=True))
    centred = stream - average
    spread = lax.optimization_barrier(jnp.mean(centred * centred, axis=-1, keepdims=True))
    return (centred * lax.rsqrt(spread + 1e-05) * gain.astype(jnp.float32)).astype(jnp.bfloat16)

def widen(field, reach):
    wrapped = jnp.concatenate([field[:, -reach:], field, field[:, :reach]], axis=1)
    return jnp.pad(wrapped, ((reach, reach), (0, 0), (0, 0)))

def attend_global(queries, keys, values):
    height, breadth, channels = queries.shape
    reach = RADIUS
    span = 2 * RADIUS + 1
    key_pad = widen(keys, reach)
    value_pad = widen(values, reach)
    latitudes = jnp.arange(height, dtype=jnp.int32)
    query_heads = queries.astype(jnp.float32).reshape(height, breadth, HEADS, HEAD_DIM)
    scale = 1.0 / math.sqrt(HEAD_DIM)
    offsets = jnp.arange(span * span, dtype=jnp.int32)
    anchor = jnp.zeros((), jnp.int32)

    def score_step(carry, offset):
        down_shift = offset // span
        east_shift = offset % span
        moved = lax.dynamic_slice(key_pad, (down_shift, east_shift, anchor), (height, breadth, channels))
        scores = lax.optimization_barrier(jnp.sum(query_heads * moved.astype(jnp.float32).reshape(height, breadth, HEADS, HEAD_DIM), axis=-1)) * scale
        inside = (latitudes + down_shift - reach >= 0) & (latitudes + down_shift - reach < height)
        return (carry, jnp.where(inside[:, None, None], scores, -jnp.inf))
    unused, scores = lax.scan(score_step, jnp.zeros((), jnp.float32), offsets)
    peak = lax.optimization_barrier(jnp.max(scores, axis=0, keepdims=True))
    expos = jnp.exp(scores - peak)
    weights = (expos / lax.optimization_barrier(jnp.sum(expos, axis=0, keepdims=True))).astype(jnp.bfloat16)

    def value_step(total, item):
        offset, weight = item
        down_shift = offset // span
        east_shift = offset % span
        moved = lax.dynamic_slice(value_pad, (down_shift, east_shift, anchor), (height, breadth, channels))
        moved = moved.astype(jnp.float32).reshape(height, breadth, HEADS, HEAD_DIM)
        return (total + weight.astype(jnp.float32)[..., None] * moved, None)
    start = jnp.zeros((height, breadth, HEADS, HEAD_DIM), jnp.float32)
    total, unused = lax.scan(value_step, start, (offsets, weights))
    return total.reshape(height * breadth, channels).astype(jnp.bfloat16)

def convolve(hidden, kernel):
    height, breadth, units = hidden.shape
    wide = widen(hidden, CONV_RADIUS)
    total = jnp.zeros((height, breadth, units), jnp.float32)
    for down_shift in range(2 * CONV_RADIUS + 1):
        for east_shift in range(2 * CONV_RADIUS + 1):
            piece = wide[down_shift:down_shift + height, east_shift:east_shift + breadth]
            total = total + piece.astype(jnp.float32) * kernel[down_shift, east_shift].astype(jnp.float32)
    return total

def reference(state, attention_in, attention_out, expand_weight, depth_kernel, shrink_weight, norm_attention, norm_feedforward):
    height, breadth, channels = state.shape
    stream = state.astype(jnp.float32).reshape(height * breadth, channels)
    for layer in range(LAYERS):
        normed = normalize(stream, norm_attention[layer])
        weight_in = attention_in[layer]
        queries = jnp.dot(normed, weight_in[:, :channels], preferred_element_type=jnp.float32).astype(jnp.bfloat16)
        keys = jnp.dot(normed, weight_in[:, channels:2 * channels], preferred_element_type=jnp.float32).astype(jnp.bfloat16)
        values = jnp.dot(normed, weight_in[:, 2 * channels:], preferred_element_type=jnp.float32).astype(jnp.bfloat16)
        shape_grid = (height, breadth, channels)
        mixed = attend_global(queries.reshape(shape_grid), keys.reshape(shape_grid), values.reshape(shape_grid))
        stream = stream + jnp.dot(mixed, attention_out[layer], preferred_element_type=jnp.float32)
        normed_ff = normalize(stream, norm_feedforward[layer])
        hidden = jnp.dot(normed_ff, expand_weight[layer], preferred_element_type=jnp.float32).astype(jnp.bfloat16)
        convolved = convolve(hidden.reshape(height, breadth, -1), depth_kernel[layer])
        activated = jax.nn.gelu(convolved, approximate=False).astype(jnp.bfloat16).reshape(height * breadth, -1)
        stream = stream + jnp.dot(activated, shrink_weight[layer], preferred_element_type=jnp.float32)
    return stream.astype(jnp.bfloat16).reshape(height, breadth, channels)
```

```python
import functools
import math

import jax
import jax.numpy as jnp
import numpy as np
from jax import lax
from jax.experimental import pallas as pl
from jax.experimental.pallas import tpu as pltpu
from jax.sharding import PartitionSpec as P

BF, F32 = jnp.bfloat16, jnp.float32
D, FF = 512, 2048
RADIUS = 6
REACH = 3
LAYERS = 2
H, W = 24, 48
PH, PW = 12, 8
LH, LW = PH + 2 * REACH, PW + 2 * REACH
SLAB = 24
HALF = LH * LW // 2 + 2
CHUNK = 1024
VMEM = 56 * 2**20


def transforms():
    seen, reps = set(), []
    for a in range(LH):
        for b in range(LW):
            mirror = ((-a) % LH, (-b) % LW)
            if mirror not in seen:
                seen.add((a, b))
                reps.append((a / LH, b / LW, (1.0 if mirror == (a, b) else 2.0) / (LH * LW)))
    fa, fb, weight = np.array(reps).T[:, :, None, None]
    angle = 2 * np.pi * (fa * np.arange(LH)[:, None] + fb * np.arange(LW))
    cos, sin = np.cos(angle), np.sin(angle)
    sin[np.abs(sin) < 1e-9] = 0
    forward = np.zeros((2 * HALF, LH, SLAB))
    first = 8 - REACH
    forward[:HALF, :, first : first + LW] = cos
    forward[HALF:, :, first : first + LW] = -sin
    inverse = np.concatenate(
        [cos[:, :PH, :PW].reshape(HALF, -1).T, -sin[:, :PH, :PW].reshape(HALF, -1).T], 1
    )
    taps = np.concatenate([(cos * weight)[:, :7, :7], (sin * weight)[:, :7, :7]], 0)
    return forward.reshape(2 * HALF, -1), inverse, taps.reshape(2 * HALF, -1)


def norm(x, gain):
    c = x - jnp.mean(x, axis=-1, keepdims=True)
    return c * lax.rsqrt(jnp.mean(c * c, axis=-1, keepdims=True) + 1e-5) * gain


def gelu(x):
    return 0.5 * x * (1.0 + lax.erf(x * np.float32(1 / math.sqrt(2))))


def place_halo(wide, pieces, r):
    n, s, w, e, nw, ne, sw, se = pieces
    wide[:, 0:8, :] = jnp.zeros((H + 2 * r, 8, D), F32)
    wide[:, 8 + W :, :] = jnp.zeros((H + 2 * r, 8, D), F32)
    for rows, left, middle, right in (
        (slice(0, r), nw, n, ne),
        (slice(r, r + H), w, None, e),
        (slice(r + H, r + H + r), sw, s, se),
    ):
        wide[rows, 8 - r : 8, :] = left[...].astype(F32)
        wide[rows, 8 + W : 8 + W + r, :] = right[...].astype(F32)
        if middle is not None:
            wide[rows, 8 : 8 + W, :] = middle[...].astype(F32)


def attend_kernel(grid_height, band_ref, stream_ref, *refs):
    pieces, refs = refs[:8], refs[8:]
    (win_ref, wout_ref, ga_ref, gf_ref, out_ref, nff_ref, on_ref, os_ref, ow_ref, oe_ref) = refs[:10]
    wide, kv, q, mixed, mask = refs[10:]
    step = pl.program_id(0)
    i, j = step // 3, step % 3

    @pl.when(step == 0)
    def _():
        place_halo(wide, pieces, RADIUS)

        def own(r, c):
            y = norm(stream_ref[pl.ds(r * 6, 6)].reshape(6 * W, D), ga_ref[...])
            wide[pl.ds(r * 6 + RADIUS, 6), 8 : 8 + W, :] = y.reshape(6, W, D)
            got = jnp.dot(y.astype(BF), win_ref[:, :D], preferred_element_type=F32)
            q[pl.ds(r * 6, 6)] = (got * 0.125).astype(BF).reshape(6, W, D)
            return c

        lax.fori_loop(0, 4, own, 0)

        def pairs(r, c):
            x = wide[pl.ds(r * 6, 6)].reshape(6 * 64, D).astype(BF)
            got = jnp.dot(x, win_ref[:, D:], preferred_element_type=F32)
            kv[pl.ds(r * 6, 6)] = got.astype(BF).reshape(6, 64, 2 * D)
            return c

        lax.fori_loop(0, 6, pairs, 0)

    @pl.when(j == 0)
    def _():
        row = lax.broadcasted_iota(jnp.int32, (64, 512), 0)
        col = lax.broadcasted_iota(jnp.int32, (64, 512), 1)
        a, b, u, v = row >> 4, row & 15, col >> 5, col & 31
        lat = band_ref[0] * H + i * 4 - RADIUS + u
        ok = (u >= a) & (u <= a + 12) & (v >= b + 2) & (v <= b + 14) & (lat >= 0) & (lat < grid_height)
        mask[...] = jnp.where(ok, 0.0, -jnp.inf)

    j16 = pl.multiple_of(j * 16, 16)
    keys = kv[pl.ds(i * 4, 16), pl.ds(j16, 32), :].reshape(512, 2 * D)
    qb = q[pl.ds(i * 4, 4), pl.ds(j16, 16), :].reshape(64, D)
    head = lax.broadcasted_iota(jnp.int32, (64, 256), 1) >> 6
    outs = []
    for g in range(2):
        k, v = keys[:, g * 256 : (g + 1) * 256], keys[:, D + g * 256 : D + (g + 1) * 256]
        qg = qb[:, g * 256 : (g + 1) * 256]
        qbd = jnp.concatenate([jnp.where(head == h, qg, jnp.zeros_like(qg)) for h in range(4)], 0)
        s = lax.dot_general(qbd, k, (((1,), (1,)), ((), ())), preferred_element_type=F32)
        s = (s.reshape(4, 64, 512) + mask[...][None]).reshape(256, 512)
        p = jnp.exp(s - jnp.max(s, axis=1, keepdims=True))
        total = jnp.sum(p, axis=1, keepdims=True)
        o = jnp.dot(p.astype(BF), v, preferred_element_type=F32) * (1.0 / total)
        r = o[192:]
        for h in range(3):
            r = jnp.where(head == h, o[h * 64 : (h + 1) * 64], r)
        outs.append(r.astype(BF))
    mixed[pl.ds(i * 4, 4), pl.ds(j16, 16), :] = jnp.concatenate(outs, 1).reshape(4, 16, D)

    @pl.when(step == 17)
    def _():
        def finish(r, c):
            x = mixed[pl.ds(r * 6, 6)].reshape(6 * W, D)
            x = jnp.dot(x, wout_ref[...], preferred_element_type=F32)
            x = x + stream_ref[pl.ds(r * 6, 6)].reshape(6 * W, D)
            out_ref[pl.ds(r * 6, 6)] = x.reshape(6, W, D)
            y = norm(x, gf_ref[...]).reshape(6, W, D).astype(BF)
            nff_ref[pl.ds(r * 6, 6)] = y
            ow_ref[pl.ds(r * 6, 6)] = y[:, :REACH]
            oe_ref[pl.ds(r * 6, 6)] = y[:, W - REACH :]

            @pl.when(r == 0)
            def _():
                on_ref[...] = y[:REACH]

            @pl.when(r == 3)
            def _():
                os_ref[...] = y[6 - REACH :]

            return c

        lax.fori_loop(0, 4, finish, 0)


def whole(a):
    return pl.BlockSpec(a.shape, lambda p: (0,) * len(a.shape))


def edge_shapes(r):
    rows, cols = jax.ShapeDtypeStruct((r, W, D), BF), jax.ShapeDtypeStruct((H, r, D), BF)
    return (rows, rows, cols, cols)


def attend(grid_height, band, stream, pieces, *rest):
    outs = (jax.ShapeDtypeStruct((H, W, D), F32), jax.ShapeDtypeStruct((H, W, D), BF)) + edge_shapes(REACH)
    args = (stream, *pieces, *rest)
    return pl.pallas_call(
        functools.partial(attend_kernel, grid_height),
        grid=(18,),
        in_specs=[pl.BlockSpec(memory_space=pltpu.SMEM)] + [whole(x) for x in args],
        out_specs=[whole(o) for o in outs],
        out_shape=outs,
        scratch_shapes=[
            pltpu.VMEM((H + 2 * RADIUS, 64, D), F32),
            pltpu.VMEM((H + 2 * RADIUS, 64, 2 * D), BF),
            pltpu.VMEM((H, W, D), BF),
            pltpu.VMEM((H, W, D), BF),
            pltpu.VMEM((64, 512), F32),
        ],
        compiler_params=pltpu.CompilerParams(vmem_limit_bytes=VMEM),
        name="attend",
    )(band, *args)


def feed_kernel(last, own_ref, stream_ref, *refs):
    pieces, refs = refs[:8], refs[8:]
    forward_ref, inverse_ref, kernel_ref, expand_ref, shrink_ref, gain_ref = refs[:6]
    outs, (wide, result) = refs[6:-2], refs[-2:]
    step = pl.program_id(0)

    @pl.when(step == 0)
    def _():
        place_halo(wide, pieces, REACH)
        wide[REACH : REACH + H, 8 : 8 + W, :] = own_ref[...].astype(F32)

    j8 = pl.multiple_of(step * PW, 8)
    ts = []
    for i in range(H // PH):
        x = wide[i * PH : i * PH + LH, pl.ds(j8, SLAB), :].reshape(LH * SLAB, D).astype(BF)
        ts.append(jnp.dot(forward_ref[...], x, preferred_element_type=F32).astype(BF))
    t = jnp.concatenate(ts, 0)
    acc = stream_ref[:, pl.ds(j8, PW), :].reshape(H * PW, D)
    for n in range(FF // CHUNK):
        c = slice(n * CHUNK, (n + 1) * CHUNK)
        z = jnp.dot(t, expand_ref[:, c], preferred_element_type=F32)
        kr, ki = kernel_ref[:HALF, c], kernel_ref[HALF:, c]
        acts = []
        for i in range(H // PH):
            re, im = z[2 * i * HALF : (2 * i + 1) * HALF], z[(2 * i + 1) * HALF : 2 * (i + 1) * HALF]
            y = jnp.concatenate([(re * kr - im * ki).astype(BF), (re * ki + im * kr).astype(BF)], 0)
            conv = jnp.dot(inverse_ref[...], y, preferred_element_type=F32)
            acts.append(gelu(conv).astype(BF))
        acc = acc + jnp.dot(jnp.concatenate(acts, 0), shrink_ref[c, :], preferred_element_type=F32)
    result[:, pl.ds(j8, PW), :] = acc.reshape(H, PW, D)

    @pl.when(step == W // PW - 1)
    def _():
        if last:
            outs[0][...] = result[...].astype(BF)
            return
        out_ref, on_ref, os_ref, ow_ref, oe_ref = outs
        out_ref[...] = result[...]
        for r in range(H // 6):
            y = norm(result[r * 6 : r * 6 + 6].reshape(6 * W, D), gain_ref[...]).astype(BF).reshape(6, W, D)
            if r == 0:
                on_ref[...] = y
            if r == H // 6 - 1:
                os_ref[...] = y
            ow_ref[r * 6 : r * 6 + 6] = y[:, :RADIUS]
            oe_ref[r * 6 : r * 6 + 6] = y[:, W - RADIUS :]


def feed(last, own, stream, pieces, *rest):
    if last:
        outs = (jax.ShapeDtypeStruct((H, W, D), BF),)
    else:
        outs = (jax.ShapeDtypeStruct((H, W, D), F32),) + edge_shapes(RADIUS)
    args = (own, stream, *pieces, *rest)
    return pl.pallas_call(
        functools.partial(feed_kernel, last),
        grid=(W // PW,),
        in_specs=[whole(x) for x in args],
        out_specs=[whole(o) for o in outs],
        out_shape=outs,
        scratch_shapes=[pltpu.VMEM((H + 2 * REACH, 64, D), F32), pltpu.VMEM((H, W, D), F32)],
        compiler_params=pltpu.CompilerParams(vmem_limit_bytes=VMEM),
        name="feed",
    )(*args)


def per_device(
    sizes,
    state,
    attention_in,
    attention_out,
    expand_weight,
    depth_kernel,
    shrink_weight,
    norm_attention,
    norm_feedforward,
):
    axes, nlat, nlon = sizes

    def pairs(dlat, dlon):
        def index(a, b):
            return a * nlon + b if axes[0] == "lat" else b * nlat + a

        return [
            (index(a, b), index(a + dlat, (b + dlon) % nlon))
            for a in range(nlat)
            for b in range(nlon)
            if 0 <= a + dlat < nlat
        ]

    def exchange(edges, r):
        n, s, w, e = edges

        def move(x, dlat, dlon):
            return lax.ppermute(x, axes, pairs(dlat, dlon))

        return (
            move(s, 1, 0),
            move(n, -1, 0),
            move(e, 0, 1),
            move(w, 0, -1),
            move(s[:, W - r :], 1, 1),
            move(s[:, :r], 1, -1),
            move(n[:, W - r :], -1, 1),
            move(n[:, :r], -1, -1),
        )

    forward, inverse, taps = transforms()
    forward, inverse = jnp.asarray(forward, BF), jnp.asarray(inverse, BF)
    kernels = jnp.einsum(
        "ft,ltc->lfc",
        jnp.asarray(taps, F32),
        depth_kernel.reshape(LAYERS, -1, FF).astype(F32),
        precision=lax.Precision.HIGHEST,
    )
    band = lax.axis_index("lat").astype(jnp.int32).reshape(1)
    stream = state.astype(F32)

    def normed(x):
        return norm(x.astype(F32), norm_attention[0]).astype(BF)

    edges = (
        normed(state[:RADIUS]),
        normed(state[H - RADIUS :]),
        normed(state[:, :RADIUS]),
        normed(state[:, W - RADIUS :]),
    )
    for layer in range(LAYERS):
        last = layer == LAYERS - 1
        ga, gf = norm_attention[layer][None], norm_feedforward[layer][None]
        stream, own, *edges = attend(
            nlat * H, band, stream, exchange(edges, RADIUS), attention_in[layer], attention_out[layer], ga, gf
        )
        stream, *edges = feed(
            last,
            own,
            stream,
            exchange(edges, REACH),
            forward,
            inverse,
            kernels[layer],
            expand_weight[layer],
            shrink_weight[layer],
            norm_attention[min(layer + 1, LAYERS - 1)][None],
        )
    return stream


def solution(mesh):
    in_specs = (P("lat", "lon", None), P(), P(), P(), P(), P(), P(), P())
    sizes = (tuple(mesh.axis_names), mesh.shape["lat"], mesh.shape["lon"])
    return jax.shard_map(
        functools.partial(per_device, sizes),
        mesh=mesh,
        in_specs=in_specs,
        out_specs=P("lat", "lon", None),
        check_vma=False,
    )
```

```python
import functools
import math

import jax
import jax.numpy as jnp
import numpy as np
from jax import lax
from jax.experimental import pallas as pl
from jax.experimental.pallas import tpu as pltpu
from jax.sharding import PartitionSpec as P

BF, F32 = jnp.bfloat16, jnp.float32
D, FF = 512, 2048
RADIUS = 6
REACH = 3
LAYERS = 2
H, W = 24, 48
PH, PW = 12, 8
LH, LW = PH + 2 * REACH, PW + 2 * REACH
SLAB = 24
HALF = LH * LW // 2 + 2
CHUNK = 1024
VMEM = 40 * 2**20


def transforms():
    seen, reps = set(), []
    for a in range(LH):
        for b in range(LW):
            mirror = ((-a) % LH, (-b) % LW)
            if mirror not in seen:
                seen.add((a, b))
                reps.append((a / LH, b / LW, (1.0 if mirror == (a, b) else 2.0) / (LH * LW)))
    fa, fb, weight = np.array(reps).T[:, :, None, None]
    angle = 2 * np.pi * (fa * np.arange(LH)[:, None] + fb * np.arange(LW))
    cos, sin = np.cos(angle), np.sin(angle)
    sin[np.abs(sin) < 1e-9] = 0
    forward = np.zeros((2 * HALF, LH, SLAB))
    first = 8 - REACH
    forward[:HALF, :, first : first + LW] = cos
    forward[HALF:, :, first : first + LW] = -sin
    inverse = np.concatenate(
        [cos[:, :PH, :PW].reshape(HALF, -1).T, -sin[:, :PH, :PW].reshape(HALF, -1).T], 1
    )
    taps = np.concatenate([(cos * weight)[:, :7, :7], (sin * weight)[:, :7, :7]], 0)
    return forward.reshape(2 * HALF, -1), inverse, taps.reshape(2 * HALF, -1)


def norm(x, gain):
    c = x - jnp.mean(x, axis=-1, keepdims=True)
    return c * lax.rsqrt(jnp.mean(c * c, axis=-1, keepdims=True) + 1e-5) * gain


def gelu(x):
    return 0.5 * x * (1.0 + lax.erf(x * np.float32(1 / math.sqrt(2))))


def whole(a):
    return pl.BlockSpec(a.shape, lambda p: (0,) * len(a.shape))


def of_layer(a, layer):
    return pl.BlockSpec((None,) + a.shape[1:], lambda p: (layer,) + (0,) * (len(a.shape) - 1))


def shape(*dims, dtype=BF):
    return jax.ShapeDtypeStruct(dims, dtype)


def call(body, name, grid, args, specs, outs, out_specs, scratch, cost):
    return pl.pallas_call(
        body,
        grid=(grid,),
        in_specs=specs,
        out_specs=out_specs,
        out_shape=outs,
        scratch_shapes=scratch,
        compiler_params=pltpu.CompilerParams(vmem_limit_bytes=VMEM),
        cost_estimate=pl.CostEstimate(flops=int(cost * 6e8), bytes_accessed=10**6, transcendentals=0),
        name=name,
    )(*args)


def project_kernel(x_ref, win_ref, gain_ref, q_ref, kv_ref):
    y = norm(x_ref[...].astype(F32).reshape(6 * W, D), gain_ref[...])
    q = jnp.dot(y.astype(BF), win_ref[:, :D], preferred_element_type=F32)
    q_ref[...] = (q * 0.125).astype(BF).reshape(6, W, D)
    y = y.reshape(6, W, D)[:, 8:40].reshape(6 * 32, D).astype(BF)
    kv_ref[...] = jnp.dot(y, win_ref[:, D:], preferred_element_type=F32).astype(BF).reshape(6, 32, 2 * D)


def project(layer, x, win, gains):
    def rows(width, depth):
        return pl.BlockSpec((6, width, depth), lambda p: (p, 0, 0))

    return call(
        project_kernel,
        "project",
        H // 6,
        (x, win, gains),
        [rows(W, D), of_layer(win, layer), of_layer(gains, layer)],
        (shape(H, W, D), shape(H, 32, 2 * D)),
        (rows(W, D), rows(32, 2 * D)),
        [],
        4,
    )


def fill_mask(mask, t, i, band, grid_height):
    row = lax.broadcasted_iota(jnp.int32, (64, 512), 0)
    col = lax.broadcasted_iota(jnp.int32, (64, 512), 1)
    a, b, u, v = row >> 4, row & 15, col >> 5, col & 31
    lat = band * H + i * 4 - RADIUS + u
    ok = (u >= a) & (u <= a + 12) & (v >= b + 2) & (v <= b + 14) & (lat >= 0) & (lat < grid_height)
    mask[t] = jnp.where(ok, 0.0, -jnp.inf)


def attend_block(qb, keys, mask):
    head = lax.broadcasted_iota(jnp.int32, (64, 256), 1) >> 6
    outs = []
    for g in range(2):
        k, v = keys[:, g * 256 : (g + 1) * 256], keys[:, D + g * 256 : D + (g + 1) * 256]
        qg = qb[:, g * 256 : (g + 1) * 256]
        qbd = jnp.concatenate([jnp.where(head == h, qg, jnp.zeros_like(qg)) for h in range(4)], 0)
        s = lax.dot_general(qbd, k, (((1,), (1,)), ((), ())), preferred_element_type=F32)
        s = (s.reshape(4, 64, 512) + mask[None]).reshape(256, 512)
        p = jnp.exp(s - jnp.max(s, axis=1, keepdims=True))
        total = jnp.sum(p, axis=1, keepdims=True)
        o = jnp.dot(p.astype(BF), v, preferred_element_type=F32) * (1.0 / total)
        r = o[192:]
        for h in range(3):
            r = jnp.where(head == h, o[h * 64 : (h + 1) * 64], r)
        outs.append(r.astype(BF))
    return jnp.concatenate(outs, 1)


def attend_kernel(kind, raw, bands, grid_height, band_ref, *refs):
    (q0, q1, x0, x1, wout_ref, gf_ref), refs = refs[:6], refs[6:]
    j = pl.program_id(0)
    gain = refs[0]

    def incoming(piece):
        piece = piece[...].astype(F32)
        return norm(piece, gain[...]) if raw else piece

    @pl.when(j == 0)
    def _():
        for t in range(2):
            fill_mask(refs[-1], t, bands[t], band_ref[0], grid_height)

    j16 = pl.multiple_of(j * 16, 16)
    columns = pl.ds(j16, 32)
    if kind == "inner":
        ga, win, kvm, x, w, e, xo, yo, wo, eo, kv, wide, mask = refs

        @pl.when(j == 0)
        def _():
            edge = jnp.zeros((H, 2, D), F32)
            wide[0, :, 0:2] = edge
            wide[0, :, 2:8] = incoming(w)
            wide[0, :, 8:16] = norm(x[:, 0:16].astype(F32)[:, :8], ga[...])
            wide[1, :, 0:8] = norm(x[:, 32:48].astype(F32)[:, 8:], ga[...])
            wide[1, :, 8:14] = incoming(e)
            wide[1, :, 14:16] = edge
            for side in range(2):
                y = wide[side].reshape(H * 16, D).astype(BF)
                y = jnp.dot(y, win[:, D:], preferred_element_type=F32)
                kv[:, side * 48 : side * 48 + 16] = y.astype(BF).reshape(H, 16, 2 * D)
            kv[:, 16:48] = kvm[...]

        windows = [kv[i * 4 - RADIUS : i * 4 - RADIUS + 16, columns] for i in bands]
    elif kind == "outer":
        ga, win, kv, n, s, xo, yo, wo, eo, no, so, kvh, wide, halo, mask = refs

        @pl.when(j == 0)
        def _():
            edge = jnp.zeros((12, 2, D), F32)
            wide[:, 0:2] = edge
            wide[:, 62:64] = edge
            wide[:6, 2:62] = incoming(n)
            wide[6:, 2:62] = incoming(s)
            y = wide[...].reshape(12 * 64, D).astype(BF)
            halo[...] = jnp.dot(y, win[:, D:], preferred_element_type=F32).astype(BF).reshape(12, 64, 2 * D)
            kvh[...] = halo[4:8]

        windows = [
            jnp.concatenate([halo[:6, columns], kv[:10, columns]], 0),
            jnp.concatenate([kv[14:, columns], halo[6:, columns]], 0),
        ]
    else:
        ga, kv, kvh, xo, yo, wo, eo, mask = refs
        windows = [
            jnp.concatenate([kvh[:2, columns], kv[:14, columns]], 0),
            jnp.concatenate([kv[10:, columns], kvh[2:, columns]], 0),
        ]
    mixed, old = [], []
    for t in range(2):
        qb = (q0, q1)[t][:, pl.ds(j16, 16)].reshape(64, D)
        mixed.append(attend_block(qb, windows[t].reshape(512, 2 * D), mask[t]))
        old.append((x0, x1)[t][:, pl.ds(j16, 16)].reshape(64, D).astype(F32))
    new = jnp.dot(jnp.concatenate(mixed, 0), wout_ref[...], preferred_element_type=F32)
    new = new + jnp.concatenate(old, 0)
    y = norm(new, gf_ref[...]).astype(BF).reshape(8, 16, D)
    xo[:, pl.ds(j16, 16)] = new.reshape(8, 16, D)
    yo[:, pl.ds(j16, 16)] = y

    @pl.when(j == 0)
    def _():
        wo[...] = y[:, :REACH]

    @pl.when(j == 2)
    def _():
        eo[...] = y[:, 16 - REACH :]

    if kind == "outer":

        @pl.when(j == 2)
        def _():
            no[...] = yo[:REACH]
            so[...] = yo[8 - REACH :]


def attend(kind, raw, layer, grid_height, band, q, x, wout, gf, ga, extra, cost):
    bands = {"inner": (2, 3), "outer": (0, 5), "between": (1, 4)}[kind]

    def rows(i):
        return pl.BlockSpec((4, W, D), lambda p: (i, 0, 0))

    args = (band, q, q, x, x, wout, gf, ga) + extra
    specs = [pl.BlockSpec(memory_space=pltpu.SMEM)] + [rows(bands[0]), rows(bands[1])] * 2
    specs += [of_layer(a, layer) for a in (wout, gf, ga)]
    specs += [of_layer(a, layer) if a.ndim == 3 and a.shape[0] == LAYERS else whole(a) for a in extra]
    outs = (shape(8, W, D, dtype=F32), shape(8, W, D), shape(8, REACH, D), shape(8, REACH, D))
    scratch = []
    if kind == "inner":
        outs += (shape(H, 64, 2 * D),)
        scratch += [pltpu.VMEM((2, H, 16, D), F32)]
    elif kind == "outer":
        outs += (shape(REACH, W, D), shape(REACH, W, D), shape(4, 64, 2 * D))
        scratch += [pltpu.VMEM((12, 64, D), F32), pltpu.VMEM((12, 64, 2 * D), BF)]
    scratch += [pltpu.VMEM((2, 64, 512), F32)]
    body = functools.partial(attend_kernel, kind, raw, bands, grid_height)
    return call(body, kind, 3, args, specs, outs, tuple(whole(o) for o in outs), scratch, cost)


def feed_kernel(last, *refs):
    (x_in, x_out, x_mid, y_in, y_out, y_mid, n_ref, s_ref, w_ref, e_ref), refs = refs[:10], refs[10:]
    forward_ref, inverse_ref, kernel_ref, expand_ref, shrink_ref, gain_ref = refs[:6]
    outs, (wide, result) = refs[6:-2], refs[-2:]
    step = pl.program_id(0)

    @pl.when(step == 0)
    def _():
        wide[:, 0:8] = jnp.zeros((H + 2 * REACH, 8, D), F32)
        wide[:, 8 + W :] = jnp.zeros((H + 2 * REACH, 8, D), F32)
        wide[:, 8 - REACH : 8] = w_ref[...].astype(F32)
        wide[:, 8 + W : 8 + W + REACH] = e_ref[...].astype(F32)
        first = 0
        for piece in (n_ref, y_out[:4], y_mid[:4], y_in, y_mid[4:], y_out[4:], s_ref):
            wide[first : first + piece.shape[0], 8 : 8 + W] = piece[...].astype(F32)
            first += piece.shape[0]

    j8 = pl.multiple_of(step * PW, 8)
    here = pl.ds(j8, PW)
    ts = []
    for i in range(H // PH):
        x = wide[i * PH : i * PH + LH, pl.ds(j8, SLAB), :].reshape(LH * SLAB, D).astype(BF)
        ts.append(jnp.dot(forward_ref[...], x, preferred_element_type=F32).astype(BF))
    t = jnp.concatenate(ts, 0)
    acc = [x_out[:4, here], x_mid[:4, here], x_in[:, here], x_mid[4:, here], x_out[4:, here]]
    acc = jnp.concatenate(acc, 0).reshape(H * PW, D)
    for n in range(FF // CHUNK):
        c = slice(n * CHUNK, (n + 1) * CHUNK)
        z = jnp.dot(t, expand_ref[:, c], preferred_element_type=F32)
        kr, ki = kernel_ref[:HALF, c], kernel_ref[HALF:, c]
        acts = []
        for i in range(H // PH):
            re, im = z[2 * i * HALF : (2 * i + 1) * HALF], z[(2 * i + 1) * HALF : 2 * (i + 1) * HALF]
            y = jnp.concatenate([(re * kr - im * ki).astype(BF), (re * ki + im * kr).astype(BF)], 0)
            conv = jnp.dot(inverse_ref[...], y, preferred_element_type=F32)
            acts.append(gelu(conv).astype(BF))
        acc = acc + jnp.dot(jnp.concatenate(acts, 0), shrink_ref[c, :], preferred_element_type=F32)
    result[:, here, :] = acc.reshape(H, PW, D)

    @pl.when(step == W // PW - 1)
    def _():
        if last:
            outs[0][...] = result[...].astype(BF)
            return
        out_ref, on_ref, os_ref, ow_ref, oe_ref = outs
        out_ref[...] = result[...]
        for r in range(H // 6):
            y = norm(result[r * 6 : r * 6 + 6].reshape(6 * W, D), gain_ref[...]).astype(BF).reshape(6, W, D)
            if r == 0:
                on_ref[...] = y
            if r == H // 6 - 1:
                os_ref[...] = y
            ow_ref[r * 6 : r * 6 + 6] = y[:, :RADIUS]
            oe_ref[r * 6 : r * 6 + 6] = y[:, W - RADIUS :]


def feed(last, layer, pieces, matrices, kernels, expand, shrink, gain):
    if last:
        outs = (shape(H, W, D),)
    else:
        rows, cols = shape(RADIUS, W, D), shape(H, RADIUS, D)
        outs = (shape(H, W, D, dtype=F32), rows, rows, cols, cols)
    args = (*pieces, *matrices, kernels, expand, shrink, gain)
    specs = [whole(a) for a in (*pieces, *matrices)] + [of_layer(a, layer) for a in (kernels, expand, shrink)]
    return call(
        functools.partial(feed_kernel, last),
        "feed",
        W // PW,
        args,
        specs + [whole(gain)],
        outs,
        tuple(whole(o) for o in outs),
        [pltpu.VMEM((H + 2 * REACH, 64, D), F32), pltpu.VMEM((H, W, D), F32)],
        24,
    )


def per_device(
    sizes,
    state,
    attention_in,
    attention_out,
    expand_weight,
    depth_kernel,
    shrink_weight,
    norm_attention,
    norm_feedforward,
):
    nlat, nlon = sizes
    north = [(i, i + 1) for i in range(nlat - 1)]
    south = [(b, a) for a, b in north]
    east = [(i, (i + 1) % nlon) for i in range(nlon)]
    west = [(b, a) for a, b in east]

    def trade_lat(n, s):
        return lax.ppermute(s, "lat", north), lax.ppermute(n, "lat", south)

    def trade_lon(w, e):
        return lax.ppermute(e, "lon", east), lax.ppermute(w, "lon", west)

    forward, inverse, taps = transforms()
    matrices = (jnp.asarray(forward, BF), jnp.asarray(inverse, BF))
    kernels = jnp.einsum(
        "ft,ltc->lfc",
        jnp.asarray(taps, F32),
        depth_kernel.reshape(LAYERS, -1, FF).astype(F32),
        precision=lax.Precision.HIGHEST,
    )
    band = lax.axis_index("lat").astype(jnp.int32).reshape(1)
    gains_a, gains_f = norm_attention[:, None], norm_feedforward[:, None]
    x = state
    n, s, w, e = state[:RADIUS], state[H - RADIUS :], state[:, :RADIUS], state[:, W - RADIUS :]
    for layer in range(LAYERS):
        raw = layer == 0
        last = layer == LAYERS - 1
        run = functools.partial(attend, raw=raw, layer=layer, grid_height=nlat * H, band=band, wout=attention_out)
        run = functools.partial(run, gf=gains_f, ga=gains_a, x=x)
        w, e = trade_lon(w, e)
        q, kvm = project(layer, x, attention_in, gains_a)
        n = jnp.concatenate([w[:RADIUS], n, e[:RADIUS]], 1)
        s = jnp.concatenate([w[H - RADIUS :], s, e[H - RADIUS :]], 1)
        n, s = trade_lat(n, s)
        x_in, y_in, w_in, e_in, kv = run("inner", q=q, extra=(attention_in, kvm, x, w, e), cost=8)
        x_out, y_out, w_out, e_out, no, so, kvh = run("outer", q=q, extra=(attention_in, kv, n, s), cost=8)
        n, s = trade_lat(no, so)
        x_mid, y_mid, w_mid, e_mid = run("between", q=q, extra=(kv, kvh), cost=8)
        w = jnp.concatenate([n[:, :REACH], w_out[:4], w_mid[:4], w_in, w_mid[4:], w_out[4:], s[:, :REACH]], 0)
        e = jnp.concatenate(
            [n[:, W - REACH :], e_out[:4], e_mid[:4], e_in, e_mid[4:], e_out[4:], s[:, W - REACH :]], 0
        )
        w, e = trade_lon(w, e)
        x, *edges = feed(
            last,
            layer,
            (x_in, x_out, x_mid, y_in, y_out, y_mid, n, s, w, e),
            matrices,
            kernels,
            expand_weight,
            shrink_weight,
            norm_attention[min(layer + 1, LAYERS - 1)][None],
        )
        if not last:
            n, s, w, e = edges
    return x


def solution(mesh):
    in_specs = (P("lat", "lon", None), P(), P(), P(), P(), P(), P(), P())
    sizes = (mesh.shape["lat"], mesh.shape["lon"])
    return jax.shard_map(
        functools.partial(per_device, sizes),
        mesh=mesh,
        in_specs=in_specs,
        out_specs=P("lat", "lon", None),
        check_vma=False,
    )
```

```python
import functools
import math

import jax
import jax.numpy as jnp
import numpy as np
from jax import lax
from jax.experimental import pallas as pl
from jax.experimental.pallas import tpu as pltpu
from jax.sharding import PartitionSpec as P

BF, F32 = jnp.bfloat16, jnp.float32
D, FF = 512, 2048
RADIUS = 6
REACH = 3
LAYERS = 2
H, W = 24, 48
PH, PW = 12, 8
LH, LW = PH + 2 * REACH, PW + 2 * REACH
SLAB = 24
HALF = LH * LW // 2 + 2
CHUNK = 256
PAIR = 2
PROJECT_VMEM, ATTEND_VMEM, FEED_VMEM = 12, 16, 20


def transforms():
    seen, reps = set(), []
    for a in range(LH):
        for b in range(LW):
            mirror = ((-a) % LH, (-b) % LW)
            if mirror not in seen:
                seen.add((a, b))
                reps.append((a / LH, b / LW, (1.0 if mirror == (a, b) else 2.0) / (LH * LW)))
    fa, fb, weight = np.array(reps).T[:, :, None, None]
    angle = 2 * np.pi * (fa * np.arange(LH)[:, None] + fb * np.arange(LW))
    cos, sin = np.cos(angle), np.sin(angle)
    sin[np.abs(sin) < 1e-9] = 0
    forward = np.zeros((2 * HALF, LH, SLAB))
    first = 8 - REACH
    forward[:HALF, :, first : first + LW] = cos
    forward[HALF:, :, first : first + LW] = -sin
    inverse = np.concatenate(
        [cos[:, :PH, :PW].reshape(HALF, -1).T, -sin[:, :PH, :PW].reshape(HALF, -1).T], 1
    )
    taps = np.concatenate([(cos * weight)[:, :7, :7], (sin * weight)[:, :7, :7]], 0)
    return forward.reshape(2 * HALF, -1), inverse, taps.reshape(2 * HALF, -1)


def norm(x, gain):
    c = x - jnp.mean(x, axis=-1, keepdims=True)
    return c * lax.rsqrt(jnp.mean(c * c, axis=-1, keepdims=True) + 1e-5) * gain


def gelu(x):
    return 0.5 * x * (1.0 + lax.erf(x * np.float32(1 / math.sqrt(2))))


def whole(a):
    return pl.BlockSpec(a.shape, lambda p: (0,) * len(a.shape))


def of_layer(a, layer):
    return pl.BlockSpec((None,) + a.shape[1:], lambda p: (layer,) + (0,) * (len(a.shape) - 1))


def shape(*dims, dtype=BF):
    return jax.ShapeDtypeStruct(dims, dtype)


def call(body, name, limit, grid, args, specs, outs, out_specs, scratch, cost):
    return pl.pallas_call(
        body,
        grid=(grid,),
        in_specs=specs,
        out_specs=out_specs,
        out_shape=outs,
        scratch_shapes=scratch,
        compiler_params=pltpu.CompilerParams(vmem_limit_bytes=limit * 2**20),
        cost_estimate=pl.CostEstimate(flops=int(cost * 6e8), bytes_accessed=10**6, transcendentals=0),
        name=name,
    )(*args)


def project_kernel(layer, x_ref, win_ref, gain_ref, q_ref, kv_ref):
    y = norm(x_ref[...].astype(F32).reshape(6 * W, D), gain_ref[layer : layer + 1])
    q = jnp.dot(y.astype(BF), win_ref[:, :D], preferred_element_type=F32)
    q_ref[...] = (q * np.float32(0.125 / math.log(2))).astype(BF).reshape(6, W, D)
    y = y.reshape(6, W, D)[:, 8:40].reshape(6 * 32, D).astype(BF)
    kv_ref[...] = jnp.dot(y, win_ref[:, D:], preferred_element_type=F32).astype(BF).reshape(6, 32, 2 * D)


def project(layer, x, win, gains):
    def rows(width, depth):
        return pl.BlockSpec((6, width, depth), lambda p: (p, 0, 0))

    return call(
        functools.partial(project_kernel, layer),
        "project",
        PROJECT_VMEM,
        H // 6,
        (x, win, gains),
        [rows(W, D), of_layer(win, layer), whole(gains)],
        (shape(H, W, D), shape(H, 32, 2 * D)),
        (rows(W, D), rows(32, 2 * D)),
        [],
        4,
    )


def fill_mask(mask, t, i, band, grid_height):
    row = lax.broadcasted_iota(jnp.int32, (64, 512), 0)
    col = lax.broadcasted_iota(jnp.int32, (64, 512), 1)
    a, b, u, v = row >> 4, row & 15, col >> 5, col & 31
    lat = band * H + i * 4 - RADIUS + u
    ok = (u >= a) & (u <= a + 12) & (v >= b + 2) & (v <= b + 14) & (lat >= 0) & (lat < grid_height)
    mask[t] = jnp.where(ok, 0.0, -jnp.inf)


def attend_block(qb, keys, mask):
    head = lax.broadcasted_iota(jnp.int32, (64, 256), 1) >> 6
    outs = []
    for g in range(2):
        k, v = keys[:, g * 256 : (g + 1) * 256], keys[:, D + g * 256 : D + (g + 1) * 256]
        qg = qb[:, g * 256 : (g + 1) * 256]
        qbd = jnp.concatenate([jnp.where(head == h, qg, jnp.zeros_like(qg)) for h in range(4)], 0)
        s = lax.dot_general(qbd, k, (((1,), (1,)), ((), ())), preferred_element_type=F32)
        s = (s.reshape(4, 64, 512) + mask[None]).reshape(256, 512)
        p = jnp.exp2(s - jnp.max(s, axis=1, keepdims=True))
        total = jnp.sum(p, axis=1, keepdims=True)
        o = jnp.dot(p.astype(BF), v, preferred_element_type=F32) * (1.0 / total)
        r = o[192:]
        for h in range(3):
            r = jnp.where(head == h, o[h * 64 : (h + 1) * 64], r)
        outs.append(r.astype(BF))
    return jnp.concatenate(outs, 1)


def attend_kernel(kind, layer, raw, bands, grid_height, band_ref, *refs):
    (q0, q1, x0, x1, wout_ref, gf_ref), refs = refs[:6], refs[6:]
    j = pl.program_id(0)
    gain_a, gain_f = refs[0][layer : layer + 1], gf_ref[layer : layer + 1]

    def incoming(piece):
        piece = piece[...].astype(F32)
        return norm(piece, gain_a) if raw else piece

    @pl.when(j == 0)
    def _():
        for t in range(2):
            fill_mask(refs[-1], t, bands[t], band_ref[0], grid_height)

    j16 = pl.multiple_of(j * 16, 16)
    columns = pl.ds(j16, 32)
    if kind == "inner":
        ga, win, kvm, x, w, e, xo, yo, wo, eo, kv, wide, mask = refs

        @pl.when(j == 0)
        def _():
            edge = jnp.zeros((H, 2, D), F32)
            wide[0, :, 0:2] = edge
            wide[0, :, 2:8] = incoming(w)
            wide[0, :, 8:16] = norm(x[:, 0:16].astype(F32)[:, :8], gain_a)
            wide[1, :, 0:8] = norm(x[:, 32:48].astype(F32)[:, 8:], gain_a)
            wide[1, :, 8:14] = incoming(e)
            wide[1, :, 14:16] = edge
            for side in range(2):
                y = wide[side].reshape(H * 16, D).astype(BF)
                y = jnp.dot(y, win[:, D:], preferred_element_type=F32)
                kv[:, side * 48 : side * 48 + 16] = y.astype(BF).reshape(H, 16, 2 * D)
            kv[:, 16:48] = kvm[...]

        windows = [kv[i * 4 - RADIUS : i * 4 - RADIUS + 16, columns] for i in bands]
    elif kind == "outer":
        ga, win, kv, n, s, xo, yo, wo, eo, no, so, kvh, wide, halo, mask = refs

        @pl.when(j == 0)
        def _():
            edge = jnp.zeros((12, 2, D), F32)
            wide[:, 0:2] = edge
            wide[:, 62:64] = edge
            wide[:6, 2:62] = incoming(n)
            wide[6:, 2:62] = incoming(s)
            y = wide[...].reshape(12 * 64, D).astype(BF)
            halo[...] = jnp.dot(y, win[:, D:], preferred_element_type=F32).astype(BF).reshape(12, 64, 2 * D)
            kvh[...] = halo[4:8]

        windows = [
            jnp.concatenate([halo[:6, columns], kv[:10, columns]], 0),
            jnp.concatenate([kv[14:, columns], halo[6:, columns]], 0),
        ]
    else:
        ga, kv, kvh, xo, yo, wo, eo, mask = refs
        windows = [
            jnp.concatenate([kvh[:2, columns], kv[:14, columns]], 0),
            jnp.concatenate([kv[10:, columns], kvh[2:, columns]], 0),
        ]
    mixed, old = [], []
    for t in range(2):
        qb = (q0, q1)[t][:, pl.ds(j16, 16)].reshape(64, D)
        mixed.append(attend_block(qb, windows[t].reshape(512, 2 * D), mask[t]))
        old.append((x0, x1)[t][:, pl.ds(j16, 16)].reshape(64, D).astype(F32))
    new = jnp.dot(jnp.concatenate(mixed, 0), wout_ref[...], preferred_element_type=F32)
    new = new + jnp.concatenate(old, 0)
    y = norm(new, gain_f).astype(BF).reshape(8, 16, D)
    xo[:, pl.ds(j16, 16)] = new.reshape(8, 16, D)
    yo[:, pl.ds(j16, 16)] = y

    @pl.when(j == 0)
    def _():
        wo[...] = y[:, :REACH]

    @pl.when(j == 2)
    def _():
        eo[...] = y[:, 16 - REACH :]

    if kind == "outer":

        @pl.when(j == 2)
        def _():
            no[...] = yo[:REACH]
            so[...] = yo[8 - REACH :]


def attend(kind, raw, layer, grid_height, band, q, x, wout, gf, ga, extra, cost):
    bands = {"inner": (2, 3), "outer": (0, 5), "between": (1, 4)}[kind]

    def rows(i):
        return pl.BlockSpec((4, W, D), lambda p: (i, 0, 0))

    args = (band, q, q, x, x, wout, gf, ga) + extra
    specs = [pl.BlockSpec(memory_space=pltpu.SMEM)] + [rows(bands[0]), rows(bands[1])] * 2
    specs += [of_layer(wout, layer), whole(gf), whole(ga)]
    specs += [of_layer(a, layer) if a.ndim == 3 and a.shape[0] == LAYERS else whole(a) for a in extra]
    outs = (shape(8, W, D, dtype=F32), shape(8, W, D), shape(8, REACH, D), shape(8, REACH, D))
    scratch = []
    if kind == "inner":
        outs += (shape(H, 64, 2 * D),)
        scratch += [pltpu.VMEM((2, H, 16, D), F32)]
    elif kind == "outer":
        outs += (shape(REACH, W, D), shape(REACH, W, D), shape(4, 64, 2 * D))
        scratch += [pltpu.VMEM((12, 64, D), F32), pltpu.VMEM((12, 64, 2 * D), BF)]
    scratch += [pltpu.VMEM((2, 64, 512), F32)]
    body = functools.partial(attend_kernel, kind, layer, raw, bands, grid_height)
    return call(body, kind, ATTEND_VMEM, 3, args, specs, outs, tuple(whole(o) for o in outs), scratch, cost)


def feed_kernel(layer, last, *refs):
    (x_in, x_out, x_mid, y_in, y_out, y_mid, n_ref, s_ref, w_ref, e_ref), refs = refs[:10], refs[10:]
    forward_ref, inverse_ref, kernel_ref, expand_ref, shrink_ref, gain_ref = refs[:6]
    outs, (wide, result, spectra) = refs[6:-3], refs[-3:]
    step = pl.program_id(0)

    @pl.when(step == 0)
    def _():
        wide[:, 0:8] = jnp.zeros((H + 2 * REACH, 8, D), F32)
        wide[:, 8 + W :] = jnp.zeros((H + 2 * REACH, 8, D), F32)
        wide[:, 8 - REACH : 8] = w_ref[...].astype(F32)
        wide[:, 8 + W : 8 + W + REACH] = e_ref[...].astype(F32)
        first = 0
        for piece in (n_ref, y_out[:4], y_mid[:4], y_in, y_mid[4:], y_out[4:], s_ref):
            wide[first : first + piece.shape[0], 8 : 8 + W] = piece[...].astype(F32)
            first += piece.shape[0]

    here = pl.ds(pl.multiple_of(step * PAIR * PW, PAIR * PW), PAIR * PW)
    count = PAIR * H // PH
    for c in range(PAIR):
        slab = pl.ds(pl.multiple_of((step * PAIR + c) * PW, PW), SLAB)
        for i in range(H // PH):
            x = wide[i * PH : i * PH + LH, slab, :].reshape(LH * SLAB, D).astype(BF)
            first = (c * (H // PH) + i) * 2 * HALF
            t = jnp.dot(forward_ref[...], x, preferred_element_type=F32).astype(BF)
            spectra[first : first + 2 * HALF] = t
    t = spectra[...]

    def expanded(n):
        return jnp.dot(t, expand_ref[:, n * CHUNK : (n + 1) * CHUNK], preferred_element_type=F32)

    def activated(n, z):
        c = slice(n * CHUNK, (n + 1) * CHUNK)
        kr, ki = kernel_ref[:HALF, c], kernel_ref[HALF:, c]
        acts = []
        for i in range(count):
            re, im = z[2 * i * HALF : (2 * i + 1) * HALF], z[(2 * i + 1) * HALF : 2 * (i + 1) * HALF]
            y = jnp.concatenate([(re * kr - im * ki).astype(BF), (re * ki + im * kr).astype(BF)], 0)
            acts.append(gelu(jnp.dot(inverse_ref[...], y, preferred_element_type=F32)).astype(BF))
        return jnp.concatenate(acts, 0)

    def shrunk(n, act):
        return jnp.dot(act, shrink_ref[n * CHUNK : (n + 1) * CHUNK], preferred_element_type=F32)

    acc = jnp.zeros((PAIR * H * PW, D), F32)
    z, act = expanded(0), None
    for n in range(FF // CHUNK):
        ahead = expanded(n + 1) if n + 1 < FF // CHUNK else None
        if act is not None:
            acc = acc + shrunk(n - 1, act)
        act, z = activated(n, z), ahead
    acc = acc + shrunk(FF // CHUNK - 1, act)
    old = [x_out[:4, here], x_mid[:4, here], x_in[:, here], x_mid[4:, here], x_out[4:, here]]
    old = jnp.concatenate(old, 0)
    size = H * PW
    for c in range(PAIR):
        new = acc[c * size : (c + 1) * size].reshape(H, PW, D) + old[:, c * PW : (c + 1) * PW]
        result[:, pl.ds(pl.multiple_of((step * PAIR + c) * PW, PW), PW), :] = new

    @pl.when(step == W // PW // PAIR - 1)
    def _():
        if last:
            outs[0][...] = result[...].astype(BF)
            return
        out_ref, on_ref, os_ref, ow_ref, oe_ref = outs
        out_ref[...] = result[...]
        for r in range(H // 6):
            y = norm(result[r * 6 : r * 6 + 6].reshape(6 * W, D), gain_ref[layer + 1 : layer + 2]).astype(BF).reshape(6, W, D)
            if r == 0:
                on_ref[...] = y
            if r == H // 6 - 1:
                os_ref[...] = y
            ow_ref[r * 6 : r * 6 + 6] = y[:, :RADIUS]
            oe_ref[r * 6 : r * 6 + 6] = y[:, W - RADIUS :]


def feed(last, layer, pieces, matrices, kernels, expand, shrink, gain):
    if last:
        outs = (shape(H, W, D),)
    else:
        rows, cols = shape(RADIUS, W, D), shape(H, RADIUS, D)
        outs = (shape(H, W, D, dtype=F32), rows, rows, cols, cols)
    args = (*pieces, *matrices, kernels, expand, shrink, gain)
    specs = [whole(a) for a in (*pieces, *matrices)] + [of_layer(a, layer) for a in (kernels, expand, shrink)]
    return call(
        functools.partial(feed_kernel, layer, last),
        "feed",
        FEED_VMEM,
        W // PW // PAIR,
        args,
        specs + [whole(gain)],
        outs,
        tuple(whole(o) for o in outs),
        [
            pltpu.VMEM((H + 2 * REACH, 64, D), F32),
            pltpu.VMEM((H, W, D), F32),
            pltpu.VMEM((PAIR * H // PH * 2 * HALF, D), BF),
        ],
        24,
    )


def per_device(
    sizes,
    state,
    attention_in,
    attention_out,
    expand_weight,
    depth_kernel,
    shrink_weight,
    norm_attention,
    norm_feedforward,
):
    nlat, nlon = sizes
    north = [(i, i + 1) for i in range(nlat - 1)]
    south = [(b, a) for a, b in north]
    east = [(i, (i + 1) % nlon) for i in range(nlon)]
    west = [(b, a) for a, b in east]

    def trade_lat(n, s):
        return lax.ppermute(s, "lat", north), lax.ppermute(n, "lat", south)

    def trade_lon(w, e):
        return lax.ppermute(e, "lon", east), lax.ppermute(w, "lon", west)

    forward, inverse, taps = transforms()
    matrices = (jnp.asarray(forward, BF), jnp.asarray(inverse, BF))
    kernels = jnp.einsum(
        "ft,ltc->lfc",
        jnp.asarray(taps, F32),
        depth_kernel.reshape(LAYERS, -1, FF).astype(F32),
        precision=lax.Precision.HIGHEST,
    )
    band = lax.axis_index("lat").astype(jnp.int32).reshape(1)
    gains_a, gains_f = norm_attention, norm_feedforward
    x = state
    n, s, w, e = state[:RADIUS], state[H - RADIUS :], state[:, :RADIUS], state[:, W - RADIUS :]
    for layer in range(LAYERS):
        raw = layer == 0
        last = layer == LAYERS - 1
        run = functools.partial(attend, raw=raw, layer=layer, grid_height=nlat * H, band=band, wout=attention_out)
        run = functools.partial(run, gf=gains_f, ga=gains_a, x=x)
        w, e = trade_lon(w, e)
        q, kvm = project(layer, x, attention_in, gains_a)
        n = jnp.concatenate([w[:RADIUS], n, e[:RADIUS]], 1)
        s = jnp.concatenate([w[H - RADIUS :], s, e[H - RADIUS :]], 1)
        n, s = trade_lat(n, s)
        x_in, y_in, w_in, e_in, kv = run("inner", q=q, extra=(attention_in, kvm, x, w, e), cost=8)
        x_out, y_out, w_out, e_out, no, so, kvh = run("outer", q=q, extra=(attention_in, kv, n, s), cost=8)
        n, s = trade_lat(no, so)
        x_mid, y_mid, w_mid, e_mid = run("between", q=q, extra=(kv, kvh), cost=8)
        n, s, w_out, e_out, w_mid, e_mid = lax.optimization_barrier((n, s, w_out, e_out, w_mid, e_mid))
        w = jnp.concatenate([n[:, :REACH], w_out[:4], w_mid[:4], w_in, w_mid[4:], w_out[4:], s[:, :REACH]], 0)
        e = jnp.concatenate(
            [n[:, W - REACH :], e_out[:4], e_mid[:4], e_in, e_mid[4:], e_out[4:], s[:, W - REACH :]], 0
        )
        w, e = trade_lon(w, e)
        x, *edges = feed(
            last,
            layer,
            (x_in, x_out, x_mid, y_in, y_out, y_mid, n, s, w, e),
            matrices,
            kernels,
            expand_weight,
            shrink_weight,
            gains_a,
        )
        if not last:
            n, s, w, e = edges
    return x


def solution(mesh):
    in_specs = (P("lat", "lon", None), P(), P(), P(), P(), P(), P(), P())
    sizes = (mesh.shape["lat"], mesh.shape["lon"])
    return jax.shard_map(
        functools.partial(per_device, sizes),
        mesh=mesh,
        in_specs=in_specs,
        out_specs=P("lat", "lon", None),
        check_vma=False,
    )
```

```python
import functools
import math

import jax
import jax.numpy as jnp
import numpy as np
from jax import lax
from jax.experimental import pallas as pl
from jax.experimental.pallas import tpu as pltpu
from jax.sharding import PartitionSpec as P

BF, F32 = jnp.bfloat16, jnp.float32
D, FF = 512, 2048
RADIUS = 6
REACH = 3
LAYERS = 2
H, W = 24, 48
PH, PW = 12, 8
LH, LW = PH + 2 * REACH, PW + 2 * REACH
SLAB = 24
HALF = LH * LW // 2 + 2
CHUNK = 256
PAIR = 2
PROJECT_VMEM, ATTEND_VMEM, FEED_VMEM = 12, 16, 20


def transforms():
    seen, reps = set(), []
    for a in range(LH):
        for b in range(LW):
            mirror = ((-a) % LH, (-b) % LW)
            if mirror not in seen:
                seen.add((a, b))
                reps.append((a / LH, b / LW, (1.0 if mirror == (a, b) else 2.0) / (LH * LW)))
    fa, fb, weight = np.array(reps).T[:, :, None, None]
    angle = 2 * np.pi * (fa * np.arange(LH)[:, None] + fb * np.arange(LW))
    cos, sin = np.cos(angle), np.sin(angle)
    sin[np.abs(sin) < 1e-9] = 0
    forward = np.zeros((2 * HALF, LH, SLAB))
    first = 8 - REACH
    forward[:HALF, :, first : first + LW] = cos
    forward[HALF:, :, first : first + LW] = -sin
    inverse = np.concatenate(
        [cos[:, :PH, :PW].reshape(HALF, -1).T, -sin[:, :PH, :PW].reshape(HALF, -1).T], 1
    )
    taps = np.concatenate([(cos * weight)[:, :7, :7], (sin * weight)[:, :7, :7]], 0)
    return forward.reshape(2 * HALF, -1), inverse, taps.reshape(2 * HALF, -1)


def norm(x, gain):
    c = x - jnp.mean(x, axis=-1, keepdims=True)
    return c * lax.rsqrt(jnp.mean(c * c, axis=-1, keepdims=True) + 1e-5) * gain


def gelu(x):
    return 0.5 * x * (1.0 + lax.erf(x * np.float32(1 / math.sqrt(2))))


def whole(a):
    return pl.BlockSpec(a.shape, lambda p: (0,) * len(a.shape))


def of_layer(a, layer):
    return pl.BlockSpec((None,) + a.shape[1:], lambda p: (layer,) + (0,) * (len(a.shape) - 1))


def shape(*dims, dtype=BF):
    return jax.ShapeDtypeStruct(dims, dtype)


def call(body, name, limit, grid, args, specs, outs, out_specs, scratch, cost):
    return pl.pallas_call(
        body,
        grid=(grid,),
        in_specs=specs,
        out_specs=out_specs,
        out_shape=outs,
        scratch_shapes=scratch,
        compiler_params=pltpu.CompilerParams(vmem_limit_bytes=limit * 2**20),
        cost_estimate=pl.CostEstimate(flops=int(cost * 6e8), bytes_accessed=10**6, transcendentals=0),
        name=name,
    )(*args)


def project_kernel(layer, x_ref, win_ref, gain_ref, q_ref, kv_ref):
    y = norm(x_ref[...].astype(F32).reshape(6 * W, D), gain_ref[layer : layer + 1])
    q = jnp.dot(y.astype(BF), win_ref[:, :D], preferred_element_type=F32)
    q_ref[...] = (q * np.float32(0.125 / math.log(2))).astype(BF).reshape(6, W, D)
    y = y.reshape(6, W, D)[:, 8:40].reshape(6 * 32, D).astype(BF)
    kv_ref[...] = jnp.dot(y, win_ref[:, D:], preferred_element_type=F32).astype(BF).reshape(6, 32, 2 * D)


def project(layer, x, win, gains):
    def rows(width, depth):
        return pl.BlockSpec((6, width, depth), lambda p: (p, 0, 0))

    return call(
        functools.partial(project_kernel, layer),
        "project",
        PROJECT_VMEM,
        H // 6,
        (x, win, gains),
        [rows(W, D), of_layer(win, layer), whole(gains)],
        (shape(H, W, D), shape(H, 32, 2 * D)),
        (rows(W, D), rows(32, 2 * D)),
        [],
        4,
    )


def fill_mask(mask, t, i, band, grid_height):
    row = lax.broadcasted_iota(jnp.int32, (64, 512), 0)
    col = lax.broadcasted_iota(jnp.int32, (64, 512), 1)
    a, b, u, v = row >> 4, row & 15, col >> 5, col & 31
    lat = band * H + i * 4 - RADIUS + u
    ok = (u >= a) & (u <= a + 12) & (v >= b + 2) & (v <= b + 14) & (lat >= 0) & (lat < grid_height)
    mask[t] = jnp.where(ok, 0.0, -jnp.inf)


def attend_block(qb, keys, mask):
    head = lax.broadcasted_iota(jnp.int32, (64, 256), 1) >> 6
    outs = []
    for g in range(2):
        k, v = keys[:, g * 256 : (g + 1) * 256], keys[:, D + g * 256 : D + (g + 1) * 256]
        qg = qb[:, g * 256 : (g + 1) * 256]
        qbd = jnp.concatenate([jnp.where(head == h, qg, jnp.zeros_like(qg)) for h in range(4)], 0)
        s = lax.dot_general(qbd, k, (((1,), (1,)), ((), ())), preferred_element_type=F32)
        s = (s.reshape(4, 64, 512) + mask[None]).reshape(256, 512)
        p = jnp.exp2(s - jnp.max(s, axis=1, keepdims=True))
        total = jnp.sum(p, axis=1, keepdims=True)
        o = jnp.dot(p.astype(BF), v, preferred_element_type=F32) * (1.0 / total)
        r = o[192:]
        for h in range(3):
            r = jnp.where(head == h, o[h * 64 : (h + 1) * 64], r)
        outs.append(r.astype(BF))
    return jnp.concatenate(outs, 1)


def attend_kernel(kind, layer, raw, bands, grid_height, band_ref, *refs):
    (q0, q1, x0, x1, wout_ref, gf_ref), refs = refs[:6], refs[6:]
    j = pl.program_id(0)
    gain_a, gain_f = refs[0][layer : layer + 1], gf_ref[layer : layer + 1]

    def incoming(piece):
        piece = piece[...].astype(F32)
        return norm(piece, gain_a) if raw else piece

    @pl.when(j == 0)
    def _():
        for t in range(2):
            fill_mask(refs[-1], t, bands[t], band_ref[0], grid_height)

    j16 = pl.multiple_of(j * 16, 16)
    columns = pl.ds(j16, 32)
    if kind == "inner":
        ga, win, kvm, x, w, e, xo, yo, wo, eo, kv, wide, mask = refs

        @pl.when(j == 0)
        def _():
            edge = jnp.zeros((H, 2, D), F32)
            wide[0, :, 0:2] = edge
            wide[0, :, 2:8] = incoming(w)
            wide[0, :, 8:16] = norm(x[:, 0:16].astype(F32)[:, :8], gain_a)
            wide[1, :, 0:8] = norm(x[:, 32:48].astype(F32)[:, 8:], gain_a)
            wide[1, :, 8:14] = incoming(e)
            wide[1, :, 14:16] = edge
            for side in range(2):
                y = wide[side].reshape(H * 16, D).astype(BF)
                y = jnp.dot(y, win[:, D:], preferred_element_type=F32)
                kv[:, side * 48 : side * 48 + 16] = y.astype(BF).reshape(H, 16, 2 * D)
            kv[:, 16:48] = kvm[...]

        windows = [kv[i * 4 - RADIUS : i * 4 - RADIUS + 16, columns] for i in bands]
    elif kind == "outer":
        ga, win, kv, n, s, nc, sc, xo, yo, wo, eo, no, so, kvh, wide, halo, mask = refs

        @pl.when(j == 0)
        def _():
            edge = jnp.zeros((12, 2, D), F32)
            wide[:, 0:2] = edge
            wide[:, 62:64] = edge
            for first, middle, corners in ((0, n, nc), (6, s, sc)):
                wide[first : first + 6, 8:56] = incoming(middle)
                sides = incoming(corners)
                wide[first : first + 6, 2:8] = sides[:, :6]
                wide[first : first + 6, 56:62] = sides[:, 6:]
            y = wide[...].reshape(12 * 64, D).astype(BF)
            halo[...] = jnp.dot(y, win[:, D:], preferred_element_type=F32).astype(BF).reshape(12, 64, 2 * D)
            kvh[...] = halo[4:8]

        windows = [
            jnp.concatenate([halo[:6, columns], kv[:10, columns]], 0),
            jnp.concatenate([kv[14:, columns], halo[6:, columns]], 0),
        ]
    else:
        ga, kv, kvh, xo, yo, wo, eo, mask = refs
        windows = [
            jnp.concatenate([kvh[:2, columns], kv[:14, columns]], 0),
            jnp.concatenate([kv[10:, columns], kvh[2:, columns]], 0),
        ]
    mixed, old = [], []
    for t in range(2):
        qb = (q0, q1)[t][:, pl.ds(j16, 16)].reshape(64, D)
        mixed.append(attend_block(qb, windows[t].reshape(512, 2 * D), mask[t]))
        old.append((x0, x1)[t][:, pl.ds(j16, 16)].reshape(64, D).astype(F32))
    new = jnp.dot(jnp.concatenate(mixed, 0), wout_ref[...], preferred_element_type=F32)
    new = new + jnp.concatenate(old, 0)
    y = norm(new, gain_f).astype(BF).reshape(8, 16, D)
    xo[:, pl.ds(j16, 16)] = new.reshape(8, 16, D)
    yo[:, pl.ds(j16, 16)] = y

    @pl.when(j == 0)
    def _():
        wo[...] = y[:, :REACH]

    @pl.when(j == 2)
    def _():
        eo[...] = y[:, 16 - REACH :]

    if kind == "outer":

        @pl.when(j == 2)
        def _():
            no[...] = yo[:REACH]
            so[...] = yo[8 - REACH :]


def attend(kind, raw, layer, grid_height, band, q, x, wout, gf, ga, extra, cost):
    bands = {"inner": (2, 3), "outer": (0, 5), "between": (1, 4)}[kind]

    def rows(i):
        return pl.BlockSpec((4, W, D), lambda p: (i, 0, 0))

    args = (band, q, q, x, x, wout, gf, ga) + extra
    specs = [pl.BlockSpec(memory_space=pltpu.SMEM)] + [rows(bands[0]), rows(bands[1])] * 2
    specs += [of_layer(wout, layer), whole(gf), whole(ga)]
    specs += [of_layer(a, layer) if a.ndim == 3 and a.shape[0] == LAYERS else whole(a) for a in extra]
    outs = (shape(8, W, D, dtype=F32), shape(8, W, D), shape(8, REACH, D), shape(8, REACH, D))
    scratch = []
    if kind == "inner":
        outs += (shape(H, 64, 2 * D),)
        scratch += [pltpu.VMEM((2, H, 16, D), F32)]
    elif kind == "outer":
        outs += (shape(REACH, W, D), shape(REACH, W, D), shape(4, 64, 2 * D))
        scratch += [pltpu.VMEM((12, 64, D), F32), pltpu.VMEM((12, 64, 2 * D), BF)]
    scratch += [pltpu.VMEM((2, 64, 512), F32)]
    body = functools.partial(attend_kernel, kind, layer, raw, bands, grid_height)
    return call(body, kind, ATTEND_VMEM, 3, args, specs, outs, tuple(whole(o) for o in outs), scratch, cost)


def feed_kernel(layer, last, bands, band_ref, *refs):
    (x_in, x_out, x_mid, y_in, y_out, y_mid, n_ref, s_ref, w_ref, e_ref), refs = refs[:10], refs[10:]
    forward_ref, inverse_ref, kernel_ref, expand_ref, shrink_ref, gain_ref = refs[:6]
    outs, (wide, result, spectra) = refs[6:-3], refs[-3:]
    step = pl.program_id(0)

    @pl.when(step == 0)
    def _():
        wide[:, 0:8] = jnp.zeros((H + 2 * REACH, 8, D), F32)
        wide[:, 8 + W :] = jnp.zeros((H + 2 * REACH, 8, D), F32)
        wide[:, 8 - REACH : 8] = w_ref[...].astype(F32)
        wide[:, 8 + W : 8 + W + REACH] = e_ref[...].astype(F32)
        first = 0
        for piece in (n_ref, y_out[:4], y_mid[:4], y_in, y_mid[4:], y_out[4:], s_ref):
            wide[first : first + piece.shape[0], 8 : 8 + W] = piece[...].astype(F32)
            first += piece.shape[0]

        @pl.when(band_ref[0] == 0)
        def _():
            wide[:REACH] = jnp.zeros((REACH, 64, D), F32)

        @pl.when(band_ref[0] == bands - 1)
        def _():
            wide[REACH + H :] = jnp.zeros((REACH, 64, D), F32)

    here = pl.ds(pl.multiple_of(step * PAIR * PW, PAIR * PW), PAIR * PW)
    count = PAIR * H // PH
    for c in range(PAIR):
        slab = pl.ds(pl.multiple_of((step * PAIR + c) * PW, PW), SLAB)
        for i in range(H // PH):
            x = wide[i * PH : i * PH + LH, slab, :].reshape(LH * SLAB, D).astype(BF)
            first = (c * (H // PH) + i) * 2 * HALF
            t = jnp.dot(forward_ref[...], x, preferred_element_type=F32).astype(BF)
            spectra[first : first + 2 * HALF] = t
    t = spectra[...]

    def expanded(n):
        return jnp.dot(t, expand_ref[:, n * CHUNK : (n + 1) * CHUNK], preferred_element_type=F32)

    def activated(n, z):
        c = slice(n * CHUNK, (n + 1) * CHUNK)
        kr, ki = kernel_ref[:HALF, c], kernel_ref[HALF:, c]
        acts = []
        for i in range(count):
            re, im = z[2 * i * HALF : (2 * i + 1) * HALF], z[(2 * i + 1) * HALF : 2 * (i + 1) * HALF]
            y = jnp.concatenate([(re * kr - im * ki).astype(BF), (re * ki + im * kr).astype(BF)], 0)
            acts.append(gelu(jnp.dot(inverse_ref[...], y, preferred_element_type=F32)).astype(BF))
        return jnp.concatenate(acts, 0)

    def shrunk(n, act):
        return jnp.dot(act, shrink_ref[n * CHUNK : (n + 1) * CHUNK], preferred_element_type=F32)

    acc = jnp.zeros((PAIR * H * PW, D), F32)
    z, act = expanded(0), None
    for n in range(FF // CHUNK):
        ahead = expanded(n + 1) if n + 1 < FF // CHUNK else None
        if act is not None:
            acc = acc + shrunk(n - 1, act)
        act, z = activated(n, z), ahead
    acc = acc + shrunk(FF // CHUNK - 1, act)
    old = [x_out[:4, here], x_mid[:4, here], x_in[:, here], x_mid[4:, here], x_out[4:, here]]
    old = jnp.concatenate(old, 0)
    size = H * PW
    for c in range(PAIR):
        new = acc[c * size : (c + 1) * size].reshape(H, PW, D) + old[:, c * PW : (c + 1) * PW]
        result[:, pl.ds(pl.multiple_of((step * PAIR + c) * PW, PW), PW), :] = new

    @pl.when(step == W // PW // PAIR - 1)
    def _():
        if last:
            outs[0][...] = result[...].astype(BF)
            return
        out_ref, on_ref, os_ref, ow_ref, oe_ref = outs
        out_ref[...] = result[...]
        for r in range(H // 6):
            y = norm(result[r * 6 : r * 6 + 6].reshape(6 * W, D), gain_ref[layer + 1 : layer + 2]).astype(BF).reshape(6, W, D)
            if r == 0:
                on_ref[...] = y
            if r == H // 6 - 1:
                os_ref[...] = y
            ow_ref[r * 6 : r * 6 + 6] = y[:, :RADIUS]
            oe_ref[r * 6 : r * 6 + 6] = y[:, W - RADIUS :]


def feed(last, layer, bands, band, pieces, matrices, kernels, expand, shrink, gain):
    if last:
        outs = (shape(H, W, D),)
    else:
        rows, cols = shape(RADIUS, W, D), shape(H, RADIUS, D)
        outs = (shape(H, W, D, dtype=F32), rows, rows, cols, cols)
    args = (band, *pieces, *matrices, kernels, expand, shrink, gain)
    specs = [pl.BlockSpec(memory_space=pltpu.SMEM)]
    specs += [whole(a) for a in (*pieces, *matrices)] + [of_layer(a, layer) for a in (kernels, expand, shrink)]
    return call(
        functools.partial(feed_kernel, layer, last, bands),
        "feed",
        FEED_VMEM,
        W // PW // PAIR,
        args,
        specs + [whole(gain)],
        outs,
        tuple(whole(o) for o in outs),
        [
            pltpu.VMEM((H + 2 * REACH, 64, D), F32),
            pltpu.VMEM((H, W, D), F32),
            pltpu.VMEM((PAIR * H // PH * 2 * HALF, D), BF),
        ],
        24,
    )


def per_device(
    sizes,
    state,
    attention_in,
    attention_out,
    expand_weight,
    depth_kernel,
    shrink_weight,
    norm_attention,
    norm_feedforward,
):
    nlat, nlon = sizes
    north = [(i, (i + 1) % nlat) for i in range(nlat)]
    south = [(b, a) for a, b in north]
    east = [(i, (i + 1) % nlon) for i in range(nlon)]
    west = [(b, a) for a, b in east]

    def trade_lat(n, s):
        return lax.ppermute(s, "lat", north), lax.ppermute(n, "lat", south)

    def trade_lon(w, e):
        return lax.ppermute(e, "lon", east), lax.ppermute(w, "lon", west)

    forward, inverse, taps = transforms()
    matrices = (jnp.asarray(forward, BF), jnp.asarray(inverse, BF))
    kernels = jnp.einsum(
        "ft,ltc->lfc",
        jnp.asarray(taps, F32),
        depth_kernel.reshape(LAYERS, -1, FF).astype(F32),
        precision=lax.Precision.HIGHEST,
    )
    band = lax.axis_index("lat").astype(jnp.int32).reshape(1)
    gains_a, gains_f = norm_attention, norm_feedforward
    x = state
    n, s, w, e = state[:RADIUS], state[H - RADIUS :], state[:, :RADIUS], state[:, W - RADIUS :]
    for layer in range(LAYERS):
        raw = layer == 0
        last = layer == LAYERS - 1
        run = functools.partial(attend, raw=raw, layer=layer, grid_height=nlat * H, band=band, wout=attention_out)
        run = functools.partial(run, gf=gains_f, ga=gains_a, x=x)
        w, e = trade_lon(w, e)
        n, s = trade_lat(n, s)
        q, kvm = project(layer, x, attention_in, gains_a)
        nc = jnp.concatenate([w[:RADIUS], e[:RADIUS]], 1)
        sc = jnp.concatenate([w[H - RADIUS :], e[H - RADIUS :]], 1)
        nc, sc = trade_lat(nc, sc)
        x_in, y_in, w_in, e_in, kv = run("inner", q=q, extra=(attention_in, kvm, x, w, e), cost=8)
        x_out, y_out, w_out, e_out, no, so, kvh = run("outer", q=q, extra=(attention_in, kv, n, s, nc, sc), cost=8)
        n, s = trade_lat(no, so)
        x_mid, y_mid, w_mid, e_mid = run("between", q=q, extra=(kv, kvh), cost=8)
        n, s, w_out, e_out, w_mid, e_mid = lax.optimization_barrier((n, s, w_out, e_out, w_mid, e_mid))
        w = jnp.concatenate([n[:, :REACH], w_out[:4], w_mid[:4], w_in, w_mid[4:], w_out[4:], s[:, :REACH]], 0)
        e = jnp.concatenate(
            [n[:, W - REACH :], e_out[:4], e_mid[:4], e_in, e_mid[4:], e_out[4:], s[:, W - REACH :]], 0
        )
        w, e = trade_lon(w, e)
        x, *edges = feed(
            last,
            layer,
            nlat,
            band,
            (x_in, x_out, x_mid, y_in, y_out, y_mid, n, s, w, e),
            matrices,
            kernels,
            expand_weight,
            shrink_weight,
            gains_a,
        )
        if not last:
            n, s, w, e = edges
    return x


def solution(mesh):
    in_specs = (P("lat", "lon", None), P(), P(), P(), P(), P(), P(), P())
    sizes = (mesh.shape["lat"], mesh.shape["lon"])
    return jax.shard_map(
        functools.partial(per_device, sizes),
        mesh=mesh,
        in_specs=in_specs,
        out_specs=P("lat", "lon", None),
        check_vma=False,
    )
```

```python
import functools
import math

import jax
import jax.numpy as jnp
import numpy as np
from jax import lax
from jax.experimental import pallas as pl
from jax.experimental.pallas import tpu as pltpu
from jax.sharding import PartitionSpec as P

BF, F32 = jnp.bfloat16, jnp.float32
D, FF = 512, 2048
RADIUS = 6
REACH = 3
LAYERS = 2
H, W = 24, 48
PH, PW = 12, 8
LH, LW = PH + 2 * REACH, PW + 2 * REACH
SLAB = 24
HALF = LH * LW // 2 + 2
CHUNK = 256
PAIR = 2
PROJECT_VMEM, ATTEND_VMEM, FEED_VMEM = 12, 16, 20


def transforms():
    seen, reps = set(), []
    for a in range(LH):
        for b in range(LW):
            mirror = ((-a) % LH, (-b) % LW)
            if mirror not in seen:
                seen.add((a, b))
                reps.append((a / LH, b / LW, (1.0 if mirror == (a, b) else 2.0) / (LH * LW)))
    fa, fb, weight = np.array(reps).T[:, :, None, None]
    angle = 2 * np.pi * (fa * np.arange(LH)[:, None] + fb * np.arange(LW))
    cos, sin = np.cos(angle), np.sin(angle)
    sin[np.abs(sin) < 1e-9] = 0
    forward = np.zeros((2 * HALF, LH, SLAB))
    first = 8 - REACH
    forward[:HALF, :, first : first + LW] = cos
    forward[HALF:, :, first : first + LW] = -sin
    inverse = np.concatenate(
        [cos[:, :PH, :PW].reshape(HALF, -1).T, -sin[:, :PH, :PW].reshape(HALF, -1).T], 1
    )
    taps = np.concatenate([(cos * weight)[:, :7, :7], (sin * weight)[:, :7, :7]], 0)
    return forward.reshape(2 * HALF, -1), inverse, taps.reshape(2 * HALF, -1)


def norm(x, gain):
    c = x - jnp.mean(x, axis=-1, keepdims=True)
    return c * lax.rsqrt(jnp.mean(c * c, axis=-1, keepdims=True) + 1e-5) * gain


def gelu(x):
    return 0.5 * x * (1.0 + lax.erf(x * np.float32(1 / math.sqrt(2))))


def whole(a):
    return pl.BlockSpec(a.shape, lambda p: (0,) * len(a.shape))


def of_layer(a, layer):
    return pl.BlockSpec((None,) + a.shape[1:], lambda p: (layer,) + (0,) * (len(a.shape) - 1))


def shape(*dims, dtype=BF):
    return jax.ShapeDtypeStruct(dims, dtype)


def call(body, name, limit, grid, args, specs, outs, out_specs, scratch, cost):
    return pl.pallas_call(
        body,
        grid=(grid,),
        in_specs=specs,
        out_specs=out_specs,
        out_shape=outs,
        scratch_shapes=scratch,
        compiler_params=pltpu.CompilerParams(vmem_limit_bytes=limit * 2**20),
        cost_estimate=pl.CostEstimate(flops=int(cost * 6e8), bytes_accessed=10**6, transcendentals=0),
        name=name,
    )(*args)


def project_kernel(layer, x_ref, win_ref, gain_ref, q_ref, kv_ref):
    y = norm(x_ref[...].astype(F32).reshape(6 * W, D), gain_ref[layer : layer + 1])
    q = jnp.dot(y.astype(BF), win_ref[:, :D], preferred_element_type=F32)
    q_ref[...] = (q * np.float32(0.125 / math.log(2))).astype(BF).reshape(6, W, D)
    y = y.reshape(6, W, D)[:, 8:40].reshape(6 * 32, D).astype(BF)
    kv_ref[...] = jnp.dot(y, win_ref[:, D:], preferred_element_type=F32).astype(BF).reshape(6, 32, 2 * D)


def project(layer, x, win, gains):
    def rows(width, depth):
        return pl.BlockSpec((6, width, depth), lambda p: (p, 0, 0))

    return call(
        functools.partial(project_kernel, layer),
        "project",
        PROJECT_VMEM,
        H // 6,
        (x, win, gains),
        [rows(W, D), of_layer(win, layer), whole(gains)],
        (shape(H, W, D), shape(H, 32, 2 * D)),
        (rows(W, D), rows(32, 2 * D)),
        [],
        4,
    )


def fill_mask(mask, t, i, band, grid_height):
    row = lax.broadcasted_iota(jnp.int32, (64, 512), 0)
    col = lax.broadcasted_iota(jnp.int32, (64, 512), 1)
    a, b, u, v = row >> 4, row & 15, col >> 5, col & 31
    lat = band * H + i * 4 - RADIUS + u
    ok = (u >= a) & (u <= a + 12) & (v >= b + 2) & (v <= b + 14) & (lat >= 0) & (lat < grid_height)
    mask[t] = jnp.where(ok, 0.0, -jnp.inf)


def attend_block(qb, keys, mask):
    head = lax.broadcasted_iota(jnp.int32, (64, 256), 1) >> 6
    outs = []
    for g in range(2):
        k, v = keys[:, g * 256 : (g + 1) * 256], keys[:, D + g * 256 : D + (g + 1) * 256]
        qg = qb[:, g * 256 : (g + 1) * 256]
        qbd = jnp.concatenate([jnp.where(head == h, qg, jnp.zeros_like(qg)) for h in range(4)], 0)
        s = lax.dot_general(qbd, k, (((1,), (1,)), ((), ())), preferred_element_type=F32)
        s = (s.reshape(4, 64, 512) + mask[None]).reshape(256, 512)
        p = jnp.exp2(s - jnp.max(s, axis=1, keepdims=True))
        total = jnp.sum(p, axis=1, keepdims=True)
        o = jnp.dot(p.astype(BF), v, preferred_element_type=F32) * (1.0 / total)
        r = o[192:]
        for h in range(3):
            r = jnp.where(head == h, o[h * 64 : (h + 1) * 64], r)
        outs.append(r.astype(BF))
    return jnp.concatenate(outs, 1)


def attend_kernel(kind, layer, raw, bands, grid_height, band_ref, *refs):
    (q0, q1, x0, x1, wout_ref, gf_ref), refs = refs[:6], refs[6:]
    j = pl.program_id(0)
    gain_a, gain_f = refs[0][layer : layer + 1], gf_ref[layer : layer + 1]

    def incoming(piece):
        piece = piece[...].astype(F32)
        return norm(piece, gain_a) if raw else piece

    @pl.when(j == 0)
    def _():
        for t in range(2):
            fill_mask(refs[-1], t, bands[t], band_ref[0], grid_height)

    j16 = pl.multiple_of(j * 16, 16)
    columns = pl.ds(j16, 32)
    if kind == "inner":
        ga, win, kvm, x, w, e, xo, yo, wo, eo, kv, wide, mask = refs

        @pl.when(j == 0)
        def _():
            edge = jnp.zeros((H, 2, D), F32)
            wide[0, :, 0:2] = edge
            wide[0, :, 2:8] = incoming(w)
            wide[0, :, 8:16] = norm(x[:, 0:16].astype(F32)[:, :8], gain_a)
            wide[1, :, 0:8] = norm(x[:, 32:48].astype(F32)[:, 8:], gain_a)
            wide[1, :, 8:14] = incoming(e)
            wide[1, :, 14:16] = edge
            for side in range(2):
                y = wide[side].reshape(H * 16, D).astype(BF)
                y = jnp.dot(y, win[:, D:], preferred_element_type=F32)
                kv[:, side * 48 : side * 48 + 16] = y.astype(BF).reshape(H, 16, 2 * D)
            kv[:, 16:48] = kvm[...]

        windows = [kv[i * 4 - RADIUS : i * 4 - RADIUS + 16, columns] for i in bands]
    elif kind == "outer":
        ga, win, kv, n, s, nc, sc, xo, yo, wo, eo, no, so, kvh, wide, halo, mask = refs

        @pl.when(j == 0)
        def _():
            edge = jnp.zeros((12, 2, D), F32)
            wide[:, 0:2] = edge
            wide[:, 62:64] = edge
            for first, middle, corners in ((0, n, nc), (6, s, sc)):
                wide[first : first + 6, 8:56] = incoming(middle)
                sides = incoming(corners)
                wide[first : first + 6, 2:8] = sides[:, :6]
                wide[first : first + 6, 56:62] = sides[:, 6:]
            y = wide[...].reshape(12 * 64, D).astype(BF)
            halo[...] = jnp.dot(y, win[:, D:], preferred_element_type=F32).astype(BF).reshape(12, 64, 2 * D)
            kvh[...] = halo[4:8]

        windows = [
            jnp.concatenate([halo[:6, columns], kv[:10, columns]], 0),
            jnp.concatenate([kv[14:, columns], halo[6:, columns]], 0),
        ]
    else:
        ga, kv, kvh, xo, yo, wo, eo, mask = refs
        windows = [
            jnp.concatenate([kvh[:2, columns], kv[:14, columns]], 0),
            jnp.concatenate([kv[10:, columns], kvh[2:, columns]], 0),
        ]
    mixed, old = [], []
    for t in range(2):
        qb = (q0, q1)[t][:, pl.ds(j16, 16)].reshape(64, D)
        mixed.append(attend_block(qb, windows[t].reshape(512, 2 * D), mask[t]))
        old.append((x0, x1)[t][:, pl.ds(j16, 16)].reshape(64, D).astype(F32))
    new = jnp.dot(jnp.concatenate(mixed, 0), wout_ref[...], preferred_element_type=F32)
    new = new + jnp.concatenate(old, 0)
    y = norm(new, gain_f).astype(BF).reshape(8, 16, D)
    xo[:, pl.ds(j16, 16)] = new.reshape(8, 16, D)
    yo[:, pl.ds(j16, 16)] = y

    @pl.when(j == 0)
    def _():
        wo[...] = y[:, :REACH]

    @pl.when(j == 2)
    def _():
        eo[...] = y[:, 16 - REACH :]

    if kind == "outer":

        @pl.when(j == 2)
        def _():
            no[...] = yo[:REACH]
            so[...] = yo[8 - REACH :]


def attend(kind, raw, layer, grid_height, band, q, x, wout, gf, ga, extra, cost):
    bands = {"inner": (2, 3), "outer": (0, 5), "between": (1, 4)}[kind]

    def rows(i):
        return pl.BlockSpec((4, W, D), lambda p: (i, 0, 0))

    args = (band, q, q, x, x, wout, gf, ga) + extra
    specs = [pl.BlockSpec(memory_space=pltpu.SMEM)] + [rows(bands[0]), rows(bands[1])] * 2
    specs += [of_layer(wout, layer), whole(gf), whole(ga)]
    specs += [of_layer(a, layer) if a.ndim == 3 and a.shape[0] == LAYERS else whole(a) for a in extra]
    outs = (shape(8, W, D, dtype=F32), shape(8, W, D), shape(8, REACH, D), shape(8, REACH, D))
    scratch = []
    if kind == "inner":
        outs += (shape(H, 64, 2 * D),)
        scratch += [pltpu.VMEM((2, H, 16, D), F32)]
    elif kind == "outer":
        outs += (shape(REACH, W, D), shape(REACH, W, D), shape(4, 64, 2 * D))
        scratch += [pltpu.VMEM((12, 64, D), F32), pltpu.VMEM((12, 64, 2 * D), BF)]
    scratch += [pltpu.VMEM((2, 64, 512), F32)]
    body = functools.partial(attend_kernel, kind, layer, raw, bands, grid_height)
    return call(body, kind, ATTEND_VMEM, 3, args, specs, outs, tuple(whole(o) for o in outs), scratch, cost)


def feed_kernel(layer, last, bands, band_ref, *refs):
    (x_in, x_out, x_mid, y_in, y_out, y_mid, n_ref, s_ref, w_ref, e_ref), refs = refs[:10], refs[10:]
    forward_ref, inverse_ref, kernel_ref, expand_ref, shrink_ref, gain_ref = refs[:6]
    outs, (wide, result, spectra) = refs[6:-3], refs[-3:]
    step = pl.program_id(0)

    @pl.when(step == 0)
    def _():
        wide[:, 0:8] = jnp.zeros((H + 2 * REACH, 8, D), F32)
        wide[:, 8 + W :] = jnp.zeros((H + 2 * REACH, 8, D), F32)
        wide[:, 8 - REACH : 8] = w_ref[...].astype(F32)
        wide[:, 8 + W : 8 + W + REACH] = e_ref[...].astype(F32)
        first = 0
        for piece in (n_ref, y_out[:4], y_mid[:4], y_in, y_mid[4:], y_out[4:], s_ref):
            wide[first : first + piece.shape[0], 8 : 8 + W] = piece[...].astype(F32)
            first += piece.shape[0]

        @pl.when(band_ref[0] == 0)
        def _():
            wide[:REACH] = jnp.zeros((REACH, 64, D), F32)

        @pl.when(band_ref[0] == bands - 1)
        def _():
            wide[REACH + H :] = jnp.zeros((REACH, 64, D), F32)

    here = pl.ds(pl.multiple_of(step * PAIR * PW, PAIR * PW), PAIR * PW)
    count = PAIR * H // PH
    for c in range(PAIR):
        slab = pl.ds(pl.multiple_of((step * PAIR + c) * PW, PW), SLAB)
        for i in range(H // PH):
            x = wide[i * PH : i * PH + LH, slab, :].reshape(LH * SLAB, D).astype(BF)
            first = (c * (H // PH) + i) * 2 * HALF
            t = jnp.dot(forward_ref[...], x, preferred_element_type=F32).astype(BF)
            spectra[first : first + 2 * HALF] = t
    t = spectra[...]

    def expanded(n):
        return jnp.dot(t, expand_ref[:, n * CHUNK : (n + 1) * CHUNK], preferred_element_type=F32)

    def activated(n, z):
        c = slice(n * CHUNK, (n + 1) * CHUNK)
        kr, ki = kernel_ref[:HALF, c], kernel_ref[HALF:, c]
        acts = []
        for i in range(count):
            re, im = z[2 * i * HALF : (2 * i + 1) * HALF], z[(2 * i + 1) * HALF : 2 * (i + 1) * HALF]
            y = jnp.concatenate([(re * kr - im * ki).astype(BF), (re * ki + im * kr).astype(BF)], 0)
            acts.append(gelu(jnp.dot(inverse_ref[...], y, preferred_element_type=F32)).astype(BF))
        return jnp.concatenate(acts, 0)

    def shrunk(n, act):
        return jnp.dot(act, shrink_ref[n * CHUNK : (n + 1) * CHUNK], preferred_element_type=F32)

    acc = jnp.zeros((PAIR * H * PW, D), F32)
    z, act = expanded(0), None
    for n in range(FF // CHUNK):
        ahead = expanded(n + 1) if n + 1 < FF // CHUNK else None
        if act is not None:
            acc = acc + shrunk(n - 1, act)
        act, z = activated(n, z), ahead
    acc = acc + shrunk(FF // CHUNK - 1, act)
    old = [x_out[:4, here], x_mid[:4, here], x_in[:, here], x_mid[4:, here], x_out[4:, here]]
    old = jnp.concatenate(old, 0)
    size = H * PW
    for c in range(PAIR):
        new = acc[c * size : (c + 1) * size].reshape(H, PW, D) + old[:, c * PW : (c + 1) * PW]
        result[:, pl.ds(pl.multiple_of((step * PAIR + c) * PW, PW), PW), :] = new

    @pl.when(step == W // PW // PAIR - 1)
    def _():
        if last:
            outs[0][...] = result[...].astype(BF)
            return
        out_ref, on_ref, os_ref, ow_ref, oe_ref = outs
        out_ref[...] = result[...]
        for r in range(H // 6):
            y = norm(result[r * 6 : r * 6 + 6].reshape(6 * W, D), gain_ref[layer + 1 : layer + 2]).astype(BF).reshape(6, W, D)
            if r == 0:
                on_ref[...] = y
            if r == H // 6 - 1:
                os_ref[...] = y
            ow_ref[r * 6 : r * 6 + 6] = y[:, :RADIUS]
            oe_ref[r * 6 : r * 6 + 6] = y[:, W - RADIUS :]


def feed(last, layer, bands, band, pieces, matrices, kernels, expand, shrink, gain):
    if last:
        outs = (shape(H, W, D),)
    else:
        rows, cols = shape(RADIUS, W, D), shape(H, RADIUS, D)
        outs = (shape(H, W, D, dtype=F32), rows, rows, cols, cols)
    args = (band, *pieces, *matrices, kernels, expand, shrink, gain)
    specs = [pl.BlockSpec(memory_space=pltpu.SMEM)]
    specs += [whole(a) for a in (*pieces, *matrices)] + [of_layer(a, layer) for a in (kernels, expand, shrink)]
    return call(
        functools.partial(feed_kernel, layer, last, bands),
        "feed",
        FEED_VMEM,
        W // PW // PAIR,
        args,
        specs + [whole(gain)],
        outs,
        tuple(whole(o) for o in outs),
        [
            pltpu.VMEM((H + 2 * REACH, 64, D), F32),
            pltpu.VMEM((H, W, D), F32),
            pltpu.VMEM((PAIR * H // PH * 2 * HALF, D), BF),
        ],
        24,
    )


def per_device(
    sizes,
    state,
    attention_in,
    attention_out,
    expand_weight,
    depth_kernel,
    shrink_weight,
    norm_attention,
    norm_feedforward,
):
    nlat, nlon = sizes
    north = [(i, (i + 1) % nlat) for i in range(nlat)]
    south = [(b, a) for a, b in north]
    east = [(i, (i + 1) % nlon) for i in range(nlon)]
    west = [(b, a) for a, b in east]

    def trade_lat(n, s):
        return lax.ppermute(s, "lat", north), lax.ppermute(n, "lat", south)

    def trade_lon(w, e):
        return lax.ppermute(e, "lon", east), lax.ppermute(w, "lon", west)

    forward, inverse, taps = transforms()
    matrices = (jnp.asarray(forward, BF), jnp.asarray(inverse, BF))
    kernels = jnp.einsum(
        "ft,ltc->lfc",
        jnp.asarray(taps, F32),
        depth_kernel.reshape(LAYERS, -1, FF).astype(F32),
        precision=lax.Precision.HIGHEST,
    )
    band = lax.axis_index("lat").astype(jnp.int32).reshape(1)
    gains_a, gains_f = norm_attention, norm_feedforward
    x = state
    n, s, w, e = state[:RADIUS], state[H - RADIUS :], state[:, :RADIUS], state[:, W - RADIUS :]
    for layer in range(LAYERS):
        raw = layer == 0
        last = layer == LAYERS - 1
        run = functools.partial(attend, raw=raw, layer=layer, grid_height=nlat * H, band=band, wout=attention_out)
        run = functools.partial(run, gf=gains_f, ga=gains_a, x=x)
        w, e = trade_lon(w, e)
        q, kvm = project(layer, x, attention_in, gains_a)
        n, s, q = lax.optimization_barrier((n, s, q))
        n, s = trade_lat(n, s)
        nc = jnp.concatenate([w[:RADIUS], e[:RADIUS]], 1)
        sc = jnp.concatenate([w[H - RADIUS :], e[H - RADIUS :]], 1)
        nc, sc = trade_lat(nc, sc)
        x_in, y_in, w_in, e_in, kv = run("inner", q=q, extra=(attention_in, kvm, x, w, e), cost=8)
        x_out, y_out, w_out, e_out, no, so, kvh = run("outer", q=q, extra=(attention_in, kv, n, s, nc, sc), cost=8)
        n, s = trade_lat(no, so)
        x_mid, y_mid, w_mid, e_mid = run("between", q=q, extra=(kv, kvh), cost=8)
        n, s, w_out, e_out, w_mid, e_mid = lax.optimization_barrier((n, s, w_out, e_out, w_mid, e_mid))
        w = jnp.concatenate([n[:, :REACH], w_out[:4], w_mid[:4], w_in, w_mid[4:], w_out[4:], s[:, :REACH]], 0)
        e = jnp.concatenate(
            [n[:, W - REACH :], e_out[:4], e_mid[:4], e_in, e_mid[4:], e_out[4:], s[:, W - REACH :]], 0
        )
        w, e = trade_lon(w, e)
        x, *edges = feed(
            last,
            layer,
            nlat,
            band,
            (x_in, x_out, x_mid, y_in, y_out, y_mid, n, s, w, e),
            matrices,
            kernels,
            expand_weight,
            shrink_weight,
            gains_a,
        )
        if not last:
            n, s, w, e = edges
    return x


def solution(mesh):
    in_specs = (P("lat", "lon", None), P(), P(), P(), P(), P(), P(), P())
    sizes = (mesh.shape["lat"], mesh.shape["lon"])
    return jax.shard_map(
        functools.partial(per_device, sizes),
        mesh=mesh,
        in_specs=in_specs,
        out_specs=P("lat", "lon", None),
        check_vma=False,
    )
```

```python
import functools
import math

import jax
import jax.numpy as jnp
import numpy as np
from jax import lax
from jax.experimental import pallas as pl
from jax.experimental.pallas import tpu as pltpu
from jax.sharding import PartitionSpec as P

BF, F32 = jnp.bfloat16, jnp.float32
D, FF = 512, 2048
RADIUS = 6
REACH = 3
LAYERS = 2
H, W = 24, 48
PH, PW = 12, 8
LH, LW = PH + 2 * REACH, PW + 2 * REACH
SLAB = 24
HALF = LH * LW // 2 + 2
CHUNK = 256
PAIR = 2
PROJECT_VMEM, ATTEND_VMEM, FEED_VMEM = 12, 16, 20


def transforms():
    seen, reps = set(), []
    for a in range(LH):
        for b in range(LW):
            mirror = ((-a) % LH, (-b) % LW)
            if mirror not in seen:
                seen.add((a, b))
                reps.append((a / LH, b / LW, (1.0 if mirror == (a, b) else 2.0) / (LH * LW)))
    fa, fb, weight = np.array(reps).T[:, :, None, None]
    angle = 2 * np.pi * (fa * np.arange(LH)[:, None] + fb * np.arange(LW))
    cos, sin = np.cos(angle), np.sin(angle)
    sin[np.abs(sin) < 1e-9] = 0
    forward = np.zeros((2 * HALF, LH, SLAB))
    first = 8 - REACH
    forward[:HALF, :, first : first + LW] = cos
    forward[HALF:, :, first : first + LW] = -sin
    inverse = np.concatenate(
        [cos[:, :PH, :PW].reshape(HALF, -1).T, -sin[:, :PH, :PW].reshape(HALF, -1).T], 1
    )
    taps = np.concatenate([(cos * weight)[:, :7, :7], (sin * weight)[:, :7, :7]], 0)
    return forward.reshape(2 * HALF, -1), inverse, taps.reshape(2 * HALF, -1)


def norm(x, gain):
    c = x - jnp.mean(x, axis=-1, keepdims=True)
    return c * lax.rsqrt(jnp.mean(c * c, axis=-1, keepdims=True) + 1e-5) * gain


def gelu(x):
    return 0.5 * x * (1.0 + lax.erf(x * np.float32(1 / math.sqrt(2))))


def whole(a):
    return pl.BlockSpec(a.shape, lambda p: (0,) * len(a.shape))


def of_layer(a, layer):
    return pl.BlockSpec((None,) + a.shape[1:], lambda p: (layer,) + (0,) * (len(a.shape) - 1))


def shape(*dims, dtype=BF):
    return jax.ShapeDtypeStruct(dims, dtype)


def call(body, name, limit, grid, args, specs, outs, out_specs, scratch, cost):
    return pl.pallas_call(
        body,
        grid=(grid,),
        in_specs=specs,
        out_specs=out_specs,
        out_shape=outs,
        scratch_shapes=scratch,
        compiler_params=pltpu.CompilerParams(vmem_limit_bytes=limit * 2**20),
        cost_estimate=pl.CostEstimate(flops=int(cost * 6e8), bytes_accessed=10**6, transcendentals=0),
        name=name,
    )(*args)


def project_kernel(layer, x_ref, win_ref, gain_ref, q_ref, kv_ref):
    gain = gain_ref[layer : layer + 1]
    for r in range(0, H, 6):
        rows = slice(r, r + 6)
        y = norm(x_ref[rows].astype(F32).reshape(6 * W, D), gain)
        q = jnp.dot(y.astype(BF), win_ref[:, :D], preferred_element_type=F32)
        q_ref[rows] = (q * np.float32(0.125 / math.log(2))).astype(BF).reshape(6, W, D)
        y = y.reshape(6, W, D)[:, 8:40].reshape(6 * 32, D).astype(BF)
        kv_ref[rows] = jnp.dot(y, win_ref[:, D:], preferred_element_type=F32).astype(BF).reshape(6, 32, 2 * D)


def project(layer, x, win, gains):
    outs = (shape(H, W, D), shape(H, 32, 2 * D))
    specs = [whole(x), of_layer(win, layer), whole(gains)]
    body = functools.partial(project_kernel, layer)
    return call(body, "project", PROJECT_VMEM, 1, (x, win, gains), specs, outs, tuple(whole(o) for o in outs), [], 4)


def fill_mask(mask, t, i, band, grid_height):
    row = lax.broadcasted_iota(jnp.int32, (64, 512), 0)
    col = lax.broadcasted_iota(jnp.int32, (64, 512), 1)
    a, b, u, v = row >> 4, row & 15, col >> 5, col & 31
    lat = band * H + i * 4 - RADIUS + u
    ok = (u >= a) & (u <= a + 12) & (v >= b + 2) & (v <= b + 14) & (lat >= 0) & (lat < grid_height)
    mask[t] = jnp.where(ok, 0.0, -jnp.inf)


def scores(q, k, mask):
    head = lax.broadcasted_iota(jnp.int32, (64, 256), 1) >> 6
    apart = jnp.concatenate([jnp.where(head == h, q, jnp.zeros_like(q)) for h in range(4)], 0)
    s = lax.dot_general(apart, k, (((1,), (1,)), ((), ())), preferred_element_type=F32)
    return (s.reshape(4, 64, 512) + mask[None]).reshape(256, 512)


def weighted(s, v):
    head = lax.broadcasted_iota(jnp.int32, (64, 256), 1) >> 6
    p = jnp.exp2(s - jnp.max(s, axis=1, keepdims=True))
    total = jnp.sum(p, axis=1, keepdims=True)
    o = jnp.dot(p.astype(BF), v, preferred_element_type=F32) * (1.0 / total)
    r = o[192:]
    for h in range(3):
        r = jnp.where(head == h, o[h * 64 : (h + 1) * 64], r)
    return r.astype(BF)


def attend_blocks(blocks):
    groups = [
        (qb[:, c], pairs[:, c], pairs[:, D + c.start : D + c.stop], mask)
        for qb, pairs, mask in blocks
        for c in (slice(0, 256), slice(256, 512))
    ]
    ahead, outs = scores(groups[0][0], groups[0][1], groups[0][3]), []
    for n, (_, _, v, _) in enumerate(groups):
        now = ahead
        if n + 1 < len(groups):
            q, k, _, mask = groups[n + 1]
            ahead = scores(q, k, mask)
        outs.append(weighted(now, v))
    return [jnp.concatenate(outs[n : n + 2], 1) for n in range(0, len(outs), 2)]


def attend_kernel(kind, layer, raw, bands, grid_height, band_ref, *refs):
    (q0, q1, x0, x1, wout_ref, gf_ref), refs = refs[:6], refs[6:]
    gain_a, gain_f = refs[0][layer : layer + 1], gf_ref[layer : layer + 1]

    def incoming(piece):
        piece = piece[...].astype(F32)
        return norm(piece, gain_a) if raw else piece

    def project_pairs(y, win):
        return jnp.dot(y.astype(BF), win[:, D:], preferred_element_type=F32).astype(BF)

    masks = refs[-1]
    for t in range(2):
        fill_mask(masks, t, bands[t], band_ref[0], grid_height)
    if kind == "inner":
        ga, win, kvm, x, w, e, xo, yo, wo, eo, kv, wide, _ = refs
        edge = jnp.zeros((H, 2, D), F32)
        wide[0, :, 0:2] = edge
        wide[0, :, 2:8] = incoming(w)
        wide[0, :, 8:16] = norm(x[:, 0:16].astype(F32)[:, :8], gain_a)
        wide[1, :, 0:8] = norm(x[:, 32:48].astype(F32)[:, 8:], gain_a)
        wide[1, :, 8:14] = incoming(e)
        wide[1, :, 14:16] = edge
        for side in range(2):
            y = project_pairs(wide[side].reshape(H * 16, D), win)
            kv[:, side * 48 : side * 48 + 16] = y.reshape(H, 16, 2 * D)
        kv[:, 16:48] = kvm[...]

        def window(t, c):
            return kv[bands[t] * 4 - RADIUS : bands[t] * 4 - RADIUS + 16, c]

    elif kind == "outer":
        ga, win, kv, n, s, nc, sc, xo, yo, wo, eo, no, so, kvh, wide, halo, _ = refs
        edge = jnp.zeros((12, 2, D), F32)
        wide[:, 0:2] = edge
        wide[:, 62:64] = edge
        for first, middle, corners in ((0, n, nc), (6, s, sc)):
            wide[first : first + 6, 8:56] = incoming(middle)
            sides = incoming(corners)
            wide[first : first + 6, 2:8] = sides[:, :6]
            wide[first : first + 6, 56:62] = sides[:, 6:]
        halo[...] = project_pairs(wide[...].reshape(12 * 64, D), win).reshape(12, 64, 2 * D)
        kvh[...] = halo[4:8]

        def window(t, c):
            parts = (kv[14:, c], halo[6:, c]) if t else (halo[:6, c], kv[:10, c])
            return jnp.concatenate(parts, 0)

    else:
        ga, kv, kvh, xo, yo, wo, eo, _ = refs

        def window(t, c):
            parts = (kv[10:, c], kvh[2:, c]) if t else (kvh[:2, c], kv[:14, c])
            return jnp.concatenate(parts, 0)

    blocks, old = [], []
    for j in range(3):
        for t in range(2):
            cells = slice(j * 16, j * 16 + 16)
            pairs = window(t, slice(j * 16, j * 16 + 32)).reshape(512, 2 * D)
            blocks.append(((q0, q1)[t][:, cells].reshape(64, D), pairs, masks[t]))
            old.append((x0, x1)[t][:, cells].reshape(64, D).astype(F32))
    mixed = attend_blocks(blocks)
    for j in range(3):
        cells = slice(j * 16, j * 16 + 16)
        new = jnp.dot(jnp.concatenate(mixed[2 * j : 2 * j + 2], 0), wout_ref[...], preferred_element_type=F32)
        new = new + jnp.concatenate(old[2 * j : 2 * j + 2], 0)
        y = norm(new, gain_f).astype(BF).reshape(8, 16, D)
        xo[:, cells] = new.reshape(8, 16, D)
        yo[:, cells] = y
        if j == 0:
            wo[...] = y[:, :REACH]
        if j == 2:
            eo[...] = y[:, 16 - REACH :]
    if kind == "outer":
        no[...] = yo[:REACH]
        so[...] = yo[8 - REACH :]


def attend(kind, raw, layer, grid_height, band, q, x, wout, gf, ga, extra, cost):
    bands = {"inner": (2, 3), "outer": (0, 5), "between": (1, 4)}[kind]

    def rows(i):
        return pl.BlockSpec((4, W, D), lambda p: (i, 0, 0))

    args = (band, q, q, x, x, wout, gf, ga) + extra
    specs = [pl.BlockSpec(memory_space=pltpu.SMEM)] + [rows(bands[0]), rows(bands[1])] * 2
    specs += [of_layer(wout, layer), whole(gf), whole(ga)]
    specs += [of_layer(a, layer) if a.ndim == 3 and a.shape[0] == LAYERS else whole(a) for a in extra]
    outs = (shape(8, W, D, dtype=F32), shape(8, W, D), shape(8, REACH, D), shape(8, REACH, D))
    scratch = []
    if kind == "inner":
        outs += (shape(H, 64, 2 * D),)
        scratch += [pltpu.VMEM((2, H, 16, D), F32)]
    elif kind == "outer":
        outs += (shape(REACH, W, D), shape(REACH, W, D), shape(4, 64, 2 * D))
        scratch += [pltpu.VMEM((12, 64, D), F32), pltpu.VMEM((12, 64, 2 * D), BF)]
    scratch += [pltpu.VMEM((2, 64, 512), F32)]
    body = functools.partial(attend_kernel, kind, layer, raw, bands, grid_height)
    return call(body, kind, ATTEND_VMEM, 1, args, specs, outs, tuple(whole(o) for o in outs), scratch, cost)


def feed_kernel(layer, last, bands, band_ref, *refs):
    (x_in, x_out, x_mid, y_in, y_out, y_mid, n_ref, s_ref, w_ref, e_ref), refs = refs[:10], refs[10:]
    forward_ref, inverse_ref, kernel_ref, expand_ref, shrink_ref, gain_ref = refs[:6]
    outs, (wide, result, spectra) = refs[6:-3], refs[-3:]
    step = pl.program_id(0)

    @pl.when(step == 0)
    def _():
        wide[:, 0:8] = jnp.zeros((H + 2 * REACH, 8, D), F32)
        wide[:, 8 + W :] = jnp.zeros((H + 2 * REACH, 8, D), F32)
        wide[:, 8 - REACH : 8] = w_ref[...].astype(F32)
        wide[:, 8 + W : 8 + W + REACH] = e_ref[...].astype(F32)
        first = 0
        for piece in (n_ref, y_out[:4], y_mid[:4], y_in, y_mid[4:], y_out[4:], s_ref):
            wide[first : first + piece.shape[0], 8 : 8 + W] = piece[...].astype(F32)
            first += piece.shape[0]

        @pl.when(band_ref[0] == 0)
        def _():
            wide[:REACH] = jnp.zeros((REACH, 64, D), F32)

        @pl.when(band_ref[0] == bands - 1)
        def _():
            wide[REACH + H :] = jnp.zeros((REACH, 64, D), F32)

    here = pl.ds(pl.multiple_of(step * PAIR * PW, PAIR * PW), PAIR * PW)
    count = PAIR * H // PH
    for c in range(PAIR):
        slab = pl.ds(pl.multiple_of((step * PAIR + c) * PW, PW), SLAB)
        for i in range(H // PH):
            x = wide[i * PH : i * PH + LH, slab, :].reshape(LH * SLAB, D).astype(BF)
            first = (c * (H // PH) + i) * 2 * HALF
            t = jnp.dot(forward_ref[...], x, preferred_element_type=F32).astype(BF)
            spectra[first : first + 2 * HALF] = t
    t = spectra[...]

    def expanded(n):
        return jnp.dot(t, expand_ref[:, n * CHUNK : (n + 1) * CHUNK], preferred_element_type=F32)

    def activated(n, z):
        c = slice(n * CHUNK, (n + 1) * CHUNK)
        kr, ki = kernel_ref[:HALF, c], kernel_ref[HALF:, c]
        acts = []
        for i in range(count):
            re, im = z[2 * i * HALF : (2 * i + 1) * HALF], z[(2 * i + 1) * HALF : 2 * (i + 1) * HALF]
            y = jnp.concatenate([(re * kr - im * ki).astype(BF), (re * ki + im * kr).astype(BF)], 0)
            acts.append(gelu(jnp.dot(inverse_ref[...], y, preferred_element_type=F32)).astype(BF))
        return jnp.concatenate(acts, 0)

    def shrunk(n, act):
        return jnp.dot(act, shrink_ref[n * CHUNK : (n + 1) * CHUNK], preferred_element_type=F32)

    acc = jnp.zeros((PAIR * H * PW, D), F32)
    z, act = expanded(0), None
    for n in range(FF // CHUNK):
        ahead = expanded(n + 1) if n + 1 < FF // CHUNK else None
        if act is not None:
            acc = acc + shrunk(n - 1, act)
        act, z = activated(n, z), ahead
    acc = acc + shrunk(FF // CHUNK - 1, act)
    old = [x_out[:4, here], x_mid[:4, here], x_in[:, here], x_mid[4:, here], x_out[4:, here]]
    old = jnp.concatenate(old, 0)
    size = H * PW
    for c in range(PAIR):
        new = acc[c * size : (c + 1) * size].reshape(H, PW, D) + old[:, c * PW : (c + 1) * PW]
        result[:, pl.ds(pl.multiple_of((step * PAIR + c) * PW, PW), PW), :] = new

    @pl.when(step == W // PW // PAIR - 1)
    def _():
        if last:
            outs[0][...] = result[...].astype(BF)
            return
        out_ref, on_ref, os_ref, ow_ref, oe_ref = outs
        out_ref[...] = result[...]
        for r in range(H // 6):
            y = norm(result[r * 6 : r * 6 + 6].reshape(6 * W, D), gain_ref[layer + 1 : layer + 2]).astype(BF).reshape(6, W, D)
            if r == 0:
                on_ref[...] = y
            if r == H // 6 - 1:
                os_ref[...] = y
            ow_ref[r * 6 : r * 6 + 6] = y[:, :RADIUS]
            oe_ref[r * 6 : r * 6 + 6] = y[:, W - RADIUS :]


def feed(last, layer, bands, band, pieces, matrices, kernels, expand, shrink, gain):
    if last:
        outs = (shape(H, W, D),)
    else:
        rows, cols = shape(RADIUS, W, D), shape(H, RADIUS, D)
        outs = (shape(H, W, D, dtype=F32), rows, rows, cols, cols)
    args = (band, *pieces, *matrices, kernels, expand, shrink, gain)
    specs = [pl.BlockSpec(memory_space=pltpu.SMEM)]
    specs += [whole(a) for a in (*pieces, *matrices)] + [of_layer(a, layer) for a in (kernels, expand, shrink)]
    return call(
        functools.partial(feed_kernel, layer, last, bands),
        "feed",
        FEED_VMEM,
        W // PW // PAIR,
        args,
        specs + [whole(gain)],
        outs,
        tuple(whole(o) for o in outs),
        [
            pltpu.VMEM((H + 2 * REACH, 64, D), F32),
            pltpu.VMEM((H, W, D), F32),
            pltpu.VMEM((PAIR * H // PH * 2 * HALF, D), BF),
        ],
        24,
    )


def per_device(
    sizes,
    state,
    attention_in,
    attention_out,
    expand_weight,
    depth_kernel,
    shrink_weight,
    norm_attention,
    norm_feedforward,
):
    nlat, nlon = sizes
    north = [(i, (i + 1) % nlat) for i in range(nlat)]
    south = [(b, a) for a, b in north]
    east = [(i, (i + 1) % nlon) for i in range(nlon)]
    west = [(b, a) for a, b in east]

    def trade_lat(n, s):
        return lax.ppermute(s, "lat", north), lax.ppermute(n, "lat", south)

    def trade_lon(w, e):
        return lax.ppermute(e, "lon", east), lax.ppermute(w, "lon", west)

    forward, inverse, taps = transforms()
    matrices = (jnp.asarray(forward, BF), jnp.asarray(inverse, BF))
    kernels = jnp.einsum(
        "ft,ltc->lfc",
        jnp.asarray(taps, F32),
        depth_kernel.reshape(LAYERS, -1, FF).astype(F32),
        precision=lax.Precision.HIGHEST,
    )
    band = lax.axis_index("lat").astype(jnp.int32).reshape(1)
    gains_a, gains_f = norm_attention, norm_feedforward
    x = state
    n, s, w, e = state[:RADIUS], state[H - RADIUS :], state[:, :RADIUS], state[:, W - RADIUS :]
    for layer in range(LAYERS):
        raw = layer == 0
        last = layer == LAYERS - 1
        run = functools.partial(attend, raw=raw, layer=layer, grid_height=nlat * H, band=band, wout=attention_out)
        run = functools.partial(run, gf=gains_f, ga=gains_a, x=x)
        w, e = trade_lon(w, e)
        n, s = trade_lat(n, s)
        q, kvm = project(layer, x, attention_in, gains_a)
        nc = jnp.concatenate([w[:RADIUS], e[:RADIUS]], 1)
        sc = jnp.concatenate([w[H - RADIUS :], e[H - RADIUS :]], 1)
        nc, sc = trade_lat(nc, sc)
        x_in, y_in, w_in, e_in, kv = run("inner", q=q, extra=(attention_in, kvm, x, w, e), cost=8)
        x_out, y_out, w_out, e_out, no, so, kvh = run("outer", q=q, extra=(attention_in, kv, n, s, nc, sc), cost=8)
        n, s = trade_lat(no, so)
        x_mid, y_mid, w_mid, e_mid = run("between", q=q, extra=(kv, kvh), cost=8)
        n, s, w_out, e_out, w_mid, e_mid = lax.optimization_barrier((n, s, w_out, e_out, w_mid, e_mid))
        w = jnp.concatenate([n[:, :REACH], w_out[:4], w_mid[:4], w_in, w_mid[4:], w_out[4:], s[:, :REACH]], 0)
        e = jnp.concatenate(
            [n[:, W - REACH :], e_out[:4], e_mid[:4], e_in, e_mid[4:], e_out[4:], s[:, W - REACH :]], 0
        )
        w, e = trade_lon(w, e)
        x, *edges = feed(
            last,
            layer,
            nlat,
            band,
            (x_in, x_out, x_mid, y_in, y_out, y_mid, n, s, w, e),
            matrices,
            kernels,
            expand_weight,
            shrink_weight,
            gains_a,
        )
        if not last:
            n, s, w, e = edges
    return x


def solution(mesh):
    in_specs = (P("lat", "lon", None), P(), P(), P(), P(), P(), P(), P())
    sizes = (mesh.shape["lat"], mesh.shape["lon"])
    return jax.shard_map(
        functools.partial(per_device, sizes),
        mesh=mesh,
        in_specs=in_specs,
        out_specs=P("lat", "lon", None),
        check_vma=False,
    )
```

```python
import functools
import math

import jax
import jax.numpy as jnp
import numpy as np
from jax import lax
from jax.experimental import pallas as pl
from jax.experimental.pallas import tpu as pltpu
from jax.sharding import PartitionSpec as P

BF, F32 = jnp.bfloat16, jnp.float32
D, FF = 512, 2048
RADIUS = 6
REACH = 3
LAYERS = 2
H, W = 24, 48
PH, PW = 12, 8
LH, LW = PH + 2 * REACH, PW + 2 * REACH
SLAB = 16
SIDE = RADIUS + REACH
HALF = LH * LW // 2 + 2
CHUNK = 256
PAIR = 2
PROJECT_VMEM, FEED_VMEM = 12, 20
ATTEND_VMEM = {"inner": 18, "outer": 14, "between": 10}


def transforms():
    seen, reps = set(), []
    for a in range(LH):
        for b in range(LW):
            mirror = ((-a) % LH, (-b) % LW)
            if mirror not in seen:
                seen.add((a, b))
                reps.append((a / LH, b / LW, (1.0 if mirror == (a, b) else 2.0) / (LH * LW)))
    fa, fb, weight = np.array(reps).T[:, :, None, None]
    angle = 2 * np.pi * (fa * np.arange(LH)[:, None] + fb * np.arange(LW))
    cos, sin = np.cos(angle), np.sin(angle)
    sin[np.abs(sin) < 1e-9] = 0
    forward = np.zeros((2 * HALF, LH, SLAB))
    forward[:HALF, :, :LW] = cos
    forward[HALF:, :, :LW] = -sin
    inverse = np.concatenate(
        [cos[:, :PH, :PW].reshape(HALF, -1).T, -sin[:, :PH, :PW].reshape(HALF, -1).T], 1
    )
    taps = np.concatenate([(cos * weight)[:, :7, :7], (sin * weight)[:, :7, :7]], 0)
    return forward.reshape(2 * HALF, -1), inverse, taps.reshape(2 * HALF, -1)


def norm(x, gain):
    c = x - jnp.mean(x, axis=-1, keepdims=True)
    return c * lax.rsqrt(jnp.mean(c * c, axis=-1, keepdims=True) + 1e-5) * gain


def gelu(x):
    return 0.5 * x * (1.0 + lax.erf(x * np.float32(1 / math.sqrt(2))))


def whole(a):
    return pl.BlockSpec(a.shape, lambda p: (0,) * len(a.shape))


def of_layer(a, layer):
    return pl.BlockSpec((None,) + a.shape[1:], lambda p: (layer,) + (0,) * (len(a.shape) - 1))


def shape(*dims, dtype=BF):
    return jax.ShapeDtypeStruct(dims, dtype)


def call(body, name, limit, grid, args, specs, outs, out_specs, scratch, cost):
    return pl.pallas_call(
        body,
        grid=(grid,),
        in_specs=specs,
        out_specs=out_specs,
        out_shape=outs,
        scratch_shapes=scratch,
        compiler_params=pltpu.CompilerParams(vmem_limit_bytes=limit * 2**20),
        cost_estimate=pl.CostEstimate(flops=int(cost * 6e8), bytes_accessed=10**6, transcendentals=0),
        name=name,
    )(*args)


def write_sides(ow_ref, oe_ref, room, rows, normed, stream):
    for ref, near, inner, outer in (
        (ow_ref, slice(0, 16), slice(0, SIDE), slice(0, REACH)),
        (oe_ref, slice(W - 16, W), slice(16 - SIDE, 16), slice(16 - REACH, 16)),
    ):
        room[:6, :SIDE] = normed.astype(F32)[:, near][:, inner]
        room[:6, SIDE : SIDE + REACH] = stream[:, near][:, outer]
        ref[rows] = room[:6, : SIDE + REACH].astype(BF)


def edge_shapes():
    rows, cols = shape(RADIUS, W, D), shape(H, SIDE + REACH, D)
    return (rows, rows, cols, cols)


def edges_kernel(x_ref, gain_ref, on_ref, os_ref, ow_ref, oe_ref, room):
    for r in range(0, H, 6):
        x = x_ref[r : r + 6].astype(F32)
        y = norm(x, gain_ref[:1]).astype(BF)
        if r == 0:
            on_ref[...] = y
        if r == H - 6:
            os_ref[...] = y
        write_sides(ow_ref, oe_ref, room, slice(r, r + 6), y, x)


def first_edges(x, gains):
    outs = edge_shapes()
    room = [pltpu.VMEM((6, 16, D), F32)]
    specs, out_specs = [whole(x), whole(gains)], tuple(whole(o) for o in outs)
    return call(edges_kernel, "edges", PROJECT_VMEM, 1, (x, gains), specs, outs, out_specs, room, 1)


def scaled(q):
    return (q * np.float32(0.125 / math.log(2))).astype(BF)


def project_kernel(layer, x_ref, win_ref, gain_ref, q_ref, kv_ref):
    gain = gain_ref[layer : layer + 1]
    for r in range(0, H, 6):
        rows = slice(r, r + 6)
        y = norm(x_ref[rows].astype(F32).reshape(6 * W, D), gain).reshape(6, W, D)
        q = y[:, 16 - REACH : 48 - REACH].reshape(6 * 32, D).astype(BF)
        q_ref[rows] = scaled(jnp.dot(q, win_ref[:, :D], preferred_element_type=F32)).reshape(6, 32, D)
        y = y[:, 16 - SIDE : 48 - SIDE].reshape(6 * 32, D).astype(BF)
        kv_ref[rows] = jnp.dot(y, win_ref[:, D:], preferred_element_type=F32).astype(BF).reshape(6, 32, 2 * D)


def project(layer, x, win, gains):
    outs = (shape(H, 32, D), shape(H, 32, 2 * D))
    specs = [whole(x), of_layer(win, layer), whole(gains)]
    body = functools.partial(project_kernel, layer)
    return call(body, "project", PROJECT_VMEM, 1, (x, win, gains), specs, outs, tuple(whole(o) for o in outs), [], 0.2)


def fill_mask(mask, t, i, band, grid_height):
    row = lax.broadcasted_iota(jnp.int32, (64, 512), 0)
    col = lax.broadcasted_iota(jnp.int32, (64, 512), 1)
    a, b, u, v = row >> 4, row & 15, col >> 5, col & 31
    lat = band * H + i * 4 - RADIUS + u
    ok = (u >= a) & (u <= a + 12) & (v >= b) & (v <= b + 12) & (lat >= 0) & (lat < grid_height)
    mask[t] = jnp.where(ok, 0.0, -jnp.inf)


def scores(q, k, mask):
    head = lax.broadcasted_iota(jnp.int32, (64, 256), 1) >> 6
    apart = jnp.concatenate([jnp.where(head == h, q, jnp.zeros_like(q)) for h in range(4)], 0)
    s = lax.dot_general(apart, k, (((1,), (1,)), ((), ())), preferred_element_type=F32)
    return (s.reshape(4, 64, 512) + mask[None]).reshape(256, 512)


def weighted(s, v):
    head = lax.broadcasted_iota(jnp.int32, (64, 256), 1) >> 6
    p = jnp.exp2(s - jnp.max(s, axis=1, keepdims=True))
    total = jnp.sum(p, axis=1, keepdims=True)
    o = jnp.dot(p.astype(BF), v, preferred_element_type=F32) * (1.0 / total)
    r = o[192:]
    for h in range(3):
        r = jnp.where(head == h, o[h * 64 : (h + 1) * 64], r)
    return r.astype(BF)


def attend_blocks(blocks):
    groups = [
        (qb[:, c], pairs[:, c], pairs[:, D + c.start : D + c.stop], mask)
        for qb, pairs, mask in blocks
        for c in (slice(0, 256), slice(256, 512))
    ]
    ahead, outs = scores(groups[0][0], groups[0][1], groups[0][3]), []
    for n, (_, _, v, _) in enumerate(groups):
        now = ahead
        if n + 1 < len(groups):
            q, k, _, mask = groups[n + 1]
            ahead = scores(q, k, mask)
        outs.append(weighted(now, v))
    return [jnp.concatenate(outs[n : n + 2], 1) for n in range(0, len(outs), 2)]


def attend_kernel(kind, layer, bands, grid_height, band_ref, *refs):
    (x0, x1, w0, w1, e0, e1, wout_ref, gf_ref, ga), refs = refs[:9], refs[9:]
    gain_a, gain_f = ga[layer : layer + 1], gf_ref[layer : layer + 1]

    def project_pairs(y, win):
        return jnp.dot(y.astype(BF), win[:, D:], preferred_element_type=F32).astype(BF)

    refs, (masks, old) = refs[:-2], refs[-2:]
    for t in range(2):
        fill_mask(masks, t, bands[t], band_ref[0], grid_height)
        rows = slice(4 * t, 4 * t + 4)
        west, east = (w0, w1)[t][...].astype(F32), (e0, e1)[t][...].astype(F32)
        old[rows, :REACH] = west[:, SIDE:]
        old[rows, REACH : REACH + W] = (x0, x1)[t][...].astype(F32)
        old[rows, REACH + W : W + 2 * REACH] = east[:, SIDE:]
        old[rows, W + 2 * REACH :] = jnp.zeros((4, 64 - W - 2 * REACH, D), F32)
    if kind == "inner":
        win, qm, kvm, x, w, e, xo, yo, q, kv, wide = refs
        west = w[...].astype(F32)[:, :SIDE]
        east = e[...].astype(F32)[:, :SIDE]
        left = norm(x[:, :16].astype(F32), gain_a)
        right = norm(x[:, 32:].astype(F32), gain_a)
        wide[:, :SIDE] = west
        wide[:, SIDE:16] = left[:, : 16 - SIDE]
        wide[:, 16:25] = right[:, 16 - SIDE :]
        wide[:, 25 : 25 + SIDE] = east
        wide[:, 25 + SIDE : 48] = jnp.zeros((H, 23 - SIDE, D), F32)
        wide[:, 48 : 48 + REACH] = west[:, RADIUS:]
        wide[:, 48 + REACH : 64] = left[:, : 16 - REACH]
        wide[:, 64 : 64 + REACH] = right[:, 16 - REACH :]
        wide[:, 64 + REACH : 64 + 2 * REACH] = east[:, :REACH]
        wide[:, 64 + 2 * REACH :] = jnp.zeros((H, 16 - 2 * REACH, D), F32)
        for r in range(0, H, 12):
            rows = slice(r, r + 12)
            y = project_pairs(wide[rows, :48].reshape(12 * 48, D), win).reshape(12, 48, 2 * D)
            kv[rows, :16] = y[:, :16]
            kv[rows, 48:] = y[:, 16:]
            y = wide[rows, 48:].reshape(12 * 32, D).astype(BF)
            y = scaled(jnp.dot(y, win[:, :D], preferred_element_type=F32)).reshape(12, 32, D)
            q[rows, :16] = y[:, :16]
            q[rows, 48:] = y[:, 16:]
        kv[:, 16:48] = kvm[...]
        q[:, 16:48] = qm[...]
        qs = [q[4 * i : 4 * i + 4] for i in bands]

        def window(t, c):
            return kv[bands[t] * 4 - RADIUS : bands[t] * 4 - RADIUS + 16, c]

    elif kind == "outer":
        win, q0, q1, kv, n, s, nc, sc, xo, yo, no, so, kvh, wide, halo = refs
        qs = [q0, q1]
        wide[:, 2 * SIDE + W :] = jnp.zeros((12, 80 - 2 * SIDE - W, D), F32)
        for first, middle, corners in ((0, n, nc), (6, s, sc)):
            rows = slice(first, first + 6)
            sides = corners[...].astype(F32)
            wide[rows, :SIDE] = sides[:, :SIDE]
            wide[rows, SIDE : SIDE + W] = middle[...].astype(F32)
            wide[rows, SIDE + W : 2 * SIDE + W] = sides[:, SIDE + 1 : 2 * SIDE + 1]
        halo[...] = project_pairs(wide[...].reshape(12 * 80, D), win).reshape(12, 80, 2 * D)
        kvh[...] = halo[4:8]

        def window(t, c):
            parts = (kv[14:, c], halo[6:, c]) if t else (halo[:6, c], kv[:10, c])
            return jnp.concatenate(parts, 0)

    else:
        q0, q1, kv, kvh, xo, yo = refs
        qs = [q0, q1]

        def window(t, c):
            parts = (kv[10:, c], kvh[2:, c]) if t else (kvh[:2, c], kv[:14, c])
            return jnp.concatenate(parts, 0)

    blocks = []
    for j in range(4):
        for t in range(2):
            pairs = window(t, slice(j * 16, j * 16 + 32)).reshape(512, 2 * D)
            blocks.append((qs[t][:, j * 16 : j * 16 + 16].reshape(64, D), pairs, masks[t]))
    mixed = attend_blocks(blocks)
    for j in range(4):
        cells = slice(j * 16, j * 16 + 16)
        new = jnp.dot(jnp.concatenate(mixed[2 * j : 2 * j + 2], 0), wout_ref[...], preferred_element_type=F32)
        new = new + old[:, cells].reshape(128, D)
        xo[:, cells] = new.reshape(8, 16, D)
        yo[:, cells] = norm(new, gain_f).astype(BF).reshape(8, 16, D)
    if kind == "outer":
        no[...] = yo[:REACH, :56]
        so[...] = yo[8 - REACH :, :56]


def attend(kind, layer, grid_height, band, q, x, w, e, wout, gf, ga, extra, cost):
    bands = {"inner": (2, 3), "outer": (0, 5), "between": (1, 4)}[kind]

    def rows(a, i):
        return pl.BlockSpec((4,) + a.shape[1:], lambda p: (i, 0, 0))

    banded = (x, x, w, w, e, e)
    queries = () if kind == "inner" else (q, q)
    win = (extra[0],) if kind != "between" else ()
    rest = extra[len(win) :]
    args = (band,) + banded + (wout, gf, ga) + win + queries + rest
    specs = [pl.BlockSpec(memory_space=pltpu.SMEM)] + [rows(a, bands[n % 2]) for n, a in enumerate(banded)]
    specs += [of_layer(wout, layer), whole(gf), whole(ga)] + [of_layer(a, layer) for a in win]
    specs += [rows(a, bands[n % 2]) for n, a in enumerate(queries)] + [whole(a) for a in rest]
    outs = (shape(8, 64, D, dtype=F32), shape(8, 64, D))
    scratch = []
    if kind == "inner":
        outs += (shape(H, 64, D), shape(H, 80, 2 * D))
        scratch += [pltpu.VMEM((H, 80, D), F32)]
    elif kind == "outer":
        outs += (shape(REACH, 56, D), shape(REACH, 56, D), shape(4, 80, 2 * D))
        scratch += [pltpu.VMEM((12, 80, D), F32), pltpu.VMEM((12, 80, 2 * D), BF)]
    scratch += [pltpu.VMEM((2, 64, 512), F32), pltpu.VMEM((8, 64, D), F32)]
    body = functools.partial(attend_kernel, kind, layer, bands, grid_height)
    return call(body, kind, ATTEND_VMEM[kind], 1, args, specs, outs, tuple(whole(o) for o in outs), scratch, cost)


def feed_kernel(layer, last, bands, band_ref, *refs):
    (x_in, x_out, x_mid, y_in, y_out, y_mid, n_ref, s_ref), refs = refs[:8], refs[8:]
    forward_ref, inverse_ref, kernel_ref, expand_ref, shrink_ref, gain_ref = refs[:6]
    outs, (wide, result, spectra) = refs[6:-3], refs[-3:]
    step = pl.program_id(0)

    @pl.when(step == 0)
    def _():
        first = 0
        for piece in (n_ref, y_out[:4], y_mid[:4], y_in, y_mid[4:], y_out[4:], s_ref):
            wide[first : first + piece.shape[0], : piece.shape[1]] = piece[...].astype(F32)
            first += piece.shape[0]

        @pl.when(band_ref[0] == 0)
        def _():
            wide[:REACH] = jnp.zeros((REACH, 64, D), F32)

        @pl.when(band_ref[0] == bands - 1)
        def _():
            wide[REACH + H :] = jnp.zeros((REACH, 64, D), F32)

    count = PAIR * H // PH
    for c in range(PAIR):
        slab = pl.ds(pl.multiple_of((step * PAIR + c) * PW, PW), SLAB)
        for i in range(H // PH):
            x = wide[i * PH : i * PH + LH, slab, :].reshape(LH * SLAB, D).astype(BF)
            first = (c * (H // PH) + i) * 2 * HALF
            t = jnp.dot(forward_ref[...], x, preferred_element_type=F32).astype(BF)
            spectra[first : first + 2 * HALF] = t
    t = spectra[...]

    def expanded(n):
        return jnp.dot(t, expand_ref[:, n * CHUNK : (n + 1) * CHUNK], preferred_element_type=F32)

    def activated(n, z):
        c = slice(n * CHUNK, (n + 1) * CHUNK)
        kr, ki = kernel_ref[:HALF, c], kernel_ref[HALF:, c]
        acts = []
        for i in range(count):
            re, im = z[2 * i * HALF : (2 * i + 1) * HALF], z[(2 * i + 1) * HALF : 2 * (i + 1) * HALF]
            y = jnp.concatenate([(re * kr - im * ki).astype(BF), (re * ki + im * kr).astype(BF)], 0)
            acts.append(gelu(jnp.dot(inverse_ref[...], y, preferred_element_type=F32)).astype(BF))
        return jnp.concatenate(acts, 0)

    def shrunk(n, act):
        return jnp.dot(act, shrink_ref[n * CHUNK : (n + 1) * CHUNK], preferred_element_type=F32)

    acc = jnp.zeros((PAIR * H * PW, D), F32)
    z, act = expanded(0), None
    for n in range(FF // CHUNK):
        ahead = expanded(n + 1) if n + 1 < FF // CHUNK else None
        if act is not None:
            acc = acc + shrunk(n - 1, act)
        act, z = activated(n, z), ahead
    acc = acc + shrunk(FF // CHUNK - 1, act)
    near = pl.ds(pl.multiple_of(step * PAIR * PW, PAIR * PW), PAIR * PW + 8)
    old = [x_out[:4, near], x_mid[:4, near], x_in[:, near], x_mid[4:, near], x_out[4:, near]]
    old = jnp.concatenate(old, 0)
    size = H * PW
    for c in range(PAIR):
        new = acc[c * size : (c + 1) * size].reshape(H, PW, D) + old[:, c * PW + REACH : (c + 1) * PW + REACH]
        result[:, pl.ds(pl.multiple_of((step * PAIR + c) * PW, PW), PW), :] = new

    @pl.when(step == W // PW // PAIR - 1)
    def _():
        if last:
            outs[0][...] = result[...].astype(BF)
            return
        out_ref, on_ref, os_ref, ow_ref, oe_ref = outs
        out_ref[...] = result[...]
        for r in range(H // 6):
            y = norm(result[r * 6 : r * 6 + 6].reshape(6 * W, D), gain_ref[layer + 1 : layer + 2]).astype(BF).reshape(6, W, D)
            if r == 0:
                on_ref[...] = y
            if r == H // 6 - 1:
                os_ref[...] = y
            write_sides(ow_ref, oe_ref, wide, slice(r * 6, r * 6 + 6), y, result[r * 6 : r * 6 + 6])


def feed(last, layer, bands, band, pieces, matrices, kernels, expand, shrink, gain):
    if last:
        outs = (shape(H, W, D),)
    else:
        outs = (shape(H, W, D, dtype=F32),) + edge_shapes()
    args = (band, *pieces, *matrices, kernels, expand, shrink, gain)
    specs = [pl.BlockSpec(memory_space=pltpu.SMEM)]
    specs += [whole(a) for a in (*pieces, *matrices)] + [of_layer(a, layer) for a in (kernels, expand, shrink)]
    return call(
        functools.partial(feed_kernel, layer, last, bands),
        "feed",
        FEED_VMEM,
        W // PW // PAIR,
        args,
        specs + [whole(gain)],
        outs,
        tuple(whole(o) for o in outs),
        [
            pltpu.VMEM((H + 2 * REACH, 64, D), F32),
            pltpu.VMEM((H, W, D), F32),
            pltpu.VMEM((PAIR * H // PH * 2 * HALF, D), BF),
        ],
        24,
    )


def per_device(
    sizes,
    state,
    attention_in,
    attention_out,
    expand_weight,
    depth_kernel,
    shrink_weight,
    norm_attention,
    norm_feedforward,
):
    nlat, nlon = sizes
    north = [(i, (i + 1) % nlat) for i in range(nlat)]
    south = [(b, a) for a, b in north]
    east = [(i, (i + 1) % nlon) for i in range(nlon)]
    west = [(b, a) for a, b in east]

    def trade_lat(n, s):
        return lax.ppermute(s, "lat", north), lax.ppermute(n, "lat", south)

    def trade_lon(w, e):
        return lax.ppermute(e, "lon", east), lax.ppermute(w, "lon", west)

    forward, inverse, taps = transforms()
    matrices = (jnp.asarray(forward, BF), jnp.asarray(inverse, BF))

    band = lax.axis_index("lat").astype(jnp.int32).reshape(1)
    gains_a, gains_f = norm_attention, norm_feedforward
    x = state
    n, s, w, e = first_edges(state, gains_a)
    for layer in range(LAYERS):
        last = layer == LAYERS - 1
        w, e = trade_lon(w, e)
        n, s = trade_lat(n, s)
        qm, kvm = project(layer, x, attention_in, gains_a)
        nc = jnp.concatenate([w[:RADIUS, : SIDE + 1], e[:RADIUS, : SIDE + 1]], 1)
        sc = jnp.concatenate([w[H - RADIUS :, : SIDE + 1], e[H - RADIUS :, : SIDE + 1]], 1)
        nc, sc = trade_lat(nc, sc)
        run = functools.partial(attend, layer=layer, grid_height=nlat * H, band=band, wout=attention_out)
        run = functools.partial(run, gf=gains_f, ga=gains_a, x=x, w=w, e=e)
        x_in, y_in, q, kv = run("inner", q=None, extra=(attention_in, qm, kvm, x, w, e), cost=8)
        x_out, y_out, no, so, kvh = run("outer", q=q, extra=(attention_in, kv, n, s, nc, sc), cost=8)
        if layer == 0:
            no, so, taps_of_layers = lax.optimization_barrier((no, so, depth_kernel))
            kernels = jnp.einsum(
                "ft,ltc->lfc",
                jnp.asarray(taps, F32),
                taps_of_layers.reshape(LAYERS, -1, FF).astype(F32),
                precision=lax.Precision.HIGHEST,
            )
        n, s = trade_lat(no, so)
        x_mid, y_mid = run("between", q=q, extra=(kv, kvh), cost=8)
        x, *edges = feed(
            last,
            layer,
            nlat,
            band,
            (x_in, x_out, x_mid, y_in, y_out, y_mid, n, s),
            matrices,
            kernels,
            expand_weight,
            shrink_weight,
            gains_a,
        )
        if not last:
            n, s, w, e = edges
    return x


def solution(mesh):
    in_specs = (P("lat", "lon", None), P(), P(), P(), P(), P(), P(), P())
    sizes = (mesh.shape["lat"], mesh.shape["lon"])
    return jax.shard_map(
        functools.partial(per_device, sizes),
        mesh=mesh,
        in_specs=in_specs,
        out_specs=P("lat", "lon", None),
        check_vma=False,
    )
```

```python
import functools
import math

import jax
import jax.numpy as jnp
import numpy as np
from jax import lax
from jax.experimental import pallas as pl
from jax.experimental.pallas import tpu as pltpu
from jax.sharding import PartitionSpec as P

BF, F32 = jnp.bfloat16, jnp.float32
D, FF = 512, 2048
RADIUS = 6
REACH = 3
LAYERS = 2
H, W = 24, 48
PH, PW = 12, 8
LH, LW = PH + 2 * REACH, PW + 2 * REACH
SLAB = 16
SIDE = RADIUS + REACH
HALF = LH * LW // 2 + 2
CHUNK = 256
PAIR = 2
PROJECT_VMEM, FEED_VMEM = 12, 20
ATTEND_VMEM = {"inner": 18, "outer": 14, "between": 10}


def transforms():
    seen, reps = set(), []
    for a in range(LH):
        for b in range(LW):
            mirror = ((-a) % LH, (-b) % LW)
            if mirror not in seen:
                seen.add((a, b))
                reps.append((a / LH, b / LW, (1.0 if mirror == (a, b) else 2.0) / (LH * LW)))
    fa, fb, weight = np.array(reps).T[:, :, None, None]
    angle = 2 * np.pi * (fa * np.arange(LH)[:, None] + fb * np.arange(LW))
    cos, sin = np.cos(angle), np.sin(angle)
    sin[np.abs(sin) < 1e-9] = 0
    forward = np.zeros((2 * HALF, LH, SLAB))
    forward[:HALF, :, :LW] = cos
    forward[HALF:, :, :LW] = -sin
    inverse = np.concatenate(
        [cos[:, :PH, :PW].reshape(HALF, -1).T, -sin[:, :PH, :PW].reshape(HALF, -1).T], 1
    )
    taps = np.concatenate([(cos * weight)[:, :7, :7], (sin * weight)[:, :7, :7]], 0)
    return forward.reshape(2 * HALF, -1), inverse, taps.reshape(2 * HALF, -1)


def norm(x, gain):
    c = x - jnp.mean(x, axis=-1, keepdims=True)
    return c * lax.rsqrt(jnp.mean(c * c, axis=-1, keepdims=True) + 1e-5) * gain


def gelu(x):
    return 0.5 * x * (1.0 + lax.erf(x * np.float32(1 / math.sqrt(2))))


def whole(a):
    return pl.BlockSpec(a.shape, lambda p: (0,) * len(a.shape))


def of_layer(a, layer):
    return pl.BlockSpec((None,) + a.shape[1:], lambda p: (layer,) + (0,) * (len(a.shape) - 1))


def shape(*dims, dtype=BF):
    return jax.ShapeDtypeStruct(dims, dtype)


def call(body, name, limit, grid, args, specs, outs, out_specs, scratch, cost):
    return pl.pallas_call(
        body,
        grid=(grid,),
        in_specs=specs,
        out_specs=out_specs,
        out_shape=outs,
        scratch_shapes=scratch,
        compiler_params=pltpu.CompilerParams(vmem_limit_bytes=limit * 2**20),
        cost_estimate=pl.CostEstimate(flops=int(cost * 6e8), bytes_accessed=10**6, transcendentals=0),
        name=name,
    )(*args)


def write_sides(ow_ref, oe_ref, room, rows, normed, stream):
    for ref, near, inner, outer in (
        (ow_ref, slice(0, 16), slice(0, SIDE), slice(0, REACH)),
        (oe_ref, slice(W - 16, W), slice(16 - SIDE, 16), slice(16 - REACH, 16)),
    ):
        room[:6, :SIDE] = normed.astype(F32)[:, near][:, inner]
        room[:6, SIDE : SIDE + REACH] = stream[:, near][:, outer]
        ref[rows] = room[:6, : SIDE + REACH].astype(BF)


def edge_shapes():
    rows, cols = shape(RADIUS, W, D), shape(H, SIDE + REACH, D)
    return (rows, rows, cols, cols)


def edges_kernel(x_ref, gain_ref, on_ref, os_ref, ow_ref, oe_ref, room):
    for r in range(0, H, 6):
        x = x_ref[r : r + 6].astype(F32)
        y = norm(x, gain_ref[:1]).astype(BF)
        if r == 0:
            on_ref[...] = y
        if r == H - 6:
            os_ref[...] = y
        write_sides(ow_ref, oe_ref, room, slice(r, r + 6), y, x)


def first_edges(x, gains):
    outs = edge_shapes()
    room = [pltpu.VMEM((6, 16, D), F32)]
    specs, out_specs = [whole(x), whole(gains)], tuple(whole(o) for o in outs)
    return call(edges_kernel, "edges", PROJECT_VMEM, 1, (x, gains), specs, outs, out_specs, room, 1)


def spectra_kernel(taps_ref, kernel_ref, out_ref, room):
    for layer in range(LAYERS):
        for a in range(7):
            room[7 * a : 7 * a + 7] = kernel_ref[layer, a].astype(F32)
        room[49:] = jnp.zeros((7, FF), F32)
        for n in range(0, FF, 512):
            c = slice(n, n + 512)
            got = jnp.dot(taps_ref[...], room[:, c], precision=lax.Precision.HIGHEST, preferred_element_type=F32)
            out_ref[layer, :, c] = got


def spectra(taps, depth_kernel):
    outs = shape(LAYERS, 2 * HALF, FF, dtype=F32)
    taps = jnp.asarray(np.pad(taps, ((0, 0), (0, 7))), F32)
    args = (taps, depth_kernel)
    specs = [whole(a) for a in args]
    return call(spectra_kernel, "spectra", 16, 1, args, specs, outs, whole(outs), [pltpu.VMEM((56, FF), F32)], 1)


def corners_kernel(wn, en, ws, es, nc_ref, sc_ref, room):
    for west, east, ref in ((wn, en, nc_ref), (ws, es, sc_ref)):
        room[:, : SIDE + REACH] = west[...].astype(F32)
        room[:, SIDE + REACH : 2 * (SIDE + REACH)] = east[...].astype(F32)
        ref[...] = room[...].astype(BF)


def corners(w, e):
    def rows(i):
        return pl.BlockSpec((RADIUS,) + w.shape[1:], lambda p: (i, 0, 0))

    last = H // RADIUS - 1
    outs = (shape(RADIUS, 2 * (SIDE + REACH), D),) * 2
    specs, out_specs = [rows(0), rows(0), rows(last), rows(last)], tuple(whole(o) for o in outs)
    room = [pltpu.VMEM((RADIUS, 2 * (SIDE + REACH), D), F32)]
    return call(corners_kernel, "corners", 4, 1, (w, e, w, e), specs, outs, out_specs, room, 0.1)


def scaled(q):
    return (q * np.float32(0.125 / math.log(2))).astype(BF)


def project_kernel(layer, x_ref, win_ref, gain_ref, q_ref, kv_ref):
    gain = gain_ref[layer : layer + 1]
    for r in range(0, H, 6):
        rows = slice(r, r + 6)
        y = norm(x_ref[rows].astype(F32).reshape(6 * W, D), gain).reshape(6, W, D)
        q = y[:, 16 - REACH : 48 - REACH].reshape(6 * 32, D).astype(BF)
        q_ref[rows] = scaled(jnp.dot(q, win_ref[:, :D], preferred_element_type=F32)).reshape(6, 32, D)
        y = y[:, 16 - SIDE : 48 - SIDE].reshape(6 * 32, D).astype(BF)
        kv_ref[rows] = jnp.dot(y, win_ref[:, D:], preferred_element_type=F32).astype(BF).reshape(6, 32, 2 * D)


def project(layer, x, win, gains):
    outs = (shape(H, 32, D), shape(H, 32, 2 * D))
    specs = [whole(x), of_layer(win, layer), whole(gains)]
    body = functools.partial(project_kernel, layer)
    return call(body, "project", PROJECT_VMEM, 1, (x, win, gains), specs, outs, tuple(whole(o) for o in outs), [], 0.2)


def fill_mask(mask, t, i, band, grid_height):
    row = lax.broadcasted_iota(jnp.int32, (64, 512), 0)
    col = lax.broadcasted_iota(jnp.int32, (64, 512), 1)
    a, b, u, v = row >> 4, row & 15, col >> 5, col & 31
    lat = band * H + i * 4 - RADIUS + u
    ok = (u >= a) & (u <= a + 12) & (v >= b) & (v <= b + 12) & (lat >= 0) & (lat < grid_height)
    mask[t] = jnp.where(ok, 0.0, -jnp.inf)


def scores(q, k, mask):
    head = lax.broadcasted_iota(jnp.int32, (64, 256), 1) >> 6
    apart = jnp.concatenate([jnp.where(head == h, q, jnp.zeros_like(q)) for h in range(4)], 0)
    s = lax.dot_general(apart, k, (((1,), (1,)), ((), ())), preferred_element_type=F32)
    return (s.reshape(4, 64, 512) + mask[None]).reshape(256, 512)


def weighted(s, v):
    head = lax.broadcasted_iota(jnp.int32, (64, 256), 1) >> 6
    p = jnp.exp2(s - jnp.max(s, axis=1, keepdims=True))
    total = jnp.sum(p, axis=1, keepdims=True)
    o = jnp.dot(p.astype(BF), v, preferred_element_type=F32) * (1.0 / total)
    r = o[192:]
    for h in range(3):
        r = jnp.where(head == h, o[h * 64 : (h + 1) * 64], r)
    return r.astype(BF)


def attend_blocks(blocks):
    groups = [
        (qb[:, c], pairs[:, c], pairs[:, D + c.start : D + c.stop], mask)
        for qb, pairs, mask in blocks
        for c in (slice(0, 256), slice(256, 512))
    ]
    ahead, outs = scores(groups[0][0], groups[0][1], groups[0][3]), []
    for n, (_, _, v, _) in enumerate(groups):
        now = ahead
        if n + 1 < len(groups):
            q, k, _, mask = groups[n + 1]
            ahead = scores(q, k, mask)
        outs.append(weighted(now, v))
    return [jnp.concatenate(outs[n : n + 2], 1) for n in range(0, len(outs), 2)]


def attend_kernel(kind, layer, bands, grid_height, band_ref, *refs):
    (x0, x1, w0, w1, e0, e1, wout_ref, gf_ref, ga), refs = refs[:9], refs[9:]
    gain_a, gain_f = ga[layer : layer + 1], gf_ref[layer : layer + 1]

    def project_pairs(y, win):
        return jnp.dot(y.astype(BF), win[:, D:], preferred_element_type=F32).astype(BF)

    refs, (masks, old) = refs[:-2], refs[-2:]
    for t in range(2):
        fill_mask(masks, t, bands[t], band_ref[0], grid_height)
        rows = slice(4 * t, 4 * t + 4)
        west, east = (w0, w1)[t][...].astype(F32), (e0, e1)[t][...].astype(F32)
        old[rows, :REACH] = west[:, SIDE:]
        old[rows, REACH : REACH + W] = (x0, x1)[t][...].astype(F32)
        old[rows, REACH + W : W + 2 * REACH] = east[:, SIDE:]
        old[rows, W + 2 * REACH :] = jnp.zeros((4, 64 - W - 2 * REACH, D), F32)
    if kind == "inner":
        win, qm, kvm, x, w, e, xo, yo, q, kv, wide = refs
        west = w[...].astype(F32)[:, :SIDE]
        east = e[...].astype(F32)[:, :SIDE]
        left = norm(x[:, :16].astype(F32), gain_a)
        right = norm(x[:, 32:].astype(F32), gain_a)
        wide[:, :SIDE] = west
        wide[:, SIDE:16] = left[:, : 16 - SIDE]
        wide[:, 16:25] = right[:, 16 - SIDE :]
        wide[:, 25 : 25 + SIDE] = east
        wide[:, 25 + SIDE : 48] = jnp.zeros((H, 23 - SIDE, D), F32)
        wide[:, 48 : 48 + REACH] = west[:, RADIUS:]
        wide[:, 48 + REACH : 64] = left[:, : 16 - REACH]
        wide[:, 64 : 64 + REACH] = right[:, 16 - REACH :]
        wide[:, 64 + REACH : 64 + 2 * REACH] = east[:, :REACH]
        wide[:, 64 + 2 * REACH :] = jnp.zeros((H, 16 - 2 * REACH, D), F32)
        for r in range(0, H, 12):
            rows = slice(r, r + 12)
            y = project_pairs(wide[rows, :48].reshape(12 * 48, D), win).reshape(12, 48, 2 * D)
            kv[rows, :16] = y[:, :16]
            kv[rows, 48:] = y[:, 16:]
            y = wide[rows, 48:].reshape(12 * 32, D).astype(BF)
            y = scaled(jnp.dot(y, win[:, :D], preferred_element_type=F32)).reshape(12, 32, D)
            q[rows, :16] = y[:, :16]
            q[rows, 48:] = y[:, 16:]
        kv[:, 16:48] = kvm[...]
        q[:, 16:48] = qm[...]
        qs = [q[4 * i : 4 * i + 4] for i in bands]

        def window(t, c):
            return kv[bands[t] * 4 - RADIUS : bands[t] * 4 - RADIUS + 16, c]

    elif kind == "outer":
        win, q0, q1, kv, n, s, nc, sc, xo, yo, no, so, kvh, wide, halo = refs
        qs = [q0, q1]
        wide[:, 2 * SIDE + W :] = jnp.zeros((12, 80 - 2 * SIDE - W, D), F32)
        for first, middle, corners in ((0, n, nc), (6, s, sc)):
            rows = slice(first, first + 6)
            sides = corners[...].astype(F32)
            wide[rows, :SIDE] = sides[:, :SIDE]
            wide[rows, SIDE : SIDE + W] = middle[...].astype(F32)
            wide[rows, SIDE + W : 2 * SIDE + W] = sides[:, SIDE + REACH : 2 * SIDE + REACH]
        halo[...] = project_pairs(wide[...].reshape(12 * 80, D), win).reshape(12, 80, 2 * D)
        kvh[...] = halo[4:8]

        def window(t, c):
            parts = (kv[14:, c], halo[6:, c]) if t else (halo[:6, c], kv[:10, c])
            return jnp.concatenate(parts, 0)

    else:
        q0, q1, kv, kvh, xo, yo = refs
        qs = [q0, q1]

        def window(t, c):
            parts = (kv[10:, c], kvh[2:, c]) if t else (kvh[:2, c], kv[:14, c])
            return jnp.concatenate(parts, 0)

    blocks = []
    for j in range(4):
        for t in range(2):
            pairs = window(t, slice(j * 16, j * 16 + 32)).reshape(512, 2 * D)
            blocks.append((qs[t][:, j * 16 : j * 16 + 16].reshape(64, D), pairs, masks[t]))
    mixed = attend_blocks(blocks)
    for j in range(4):
        cells = slice(j * 16, j * 16 + 16)
        new = jnp.dot(jnp.concatenate(mixed[2 * j : 2 * j + 2], 0), wout_ref[...], preferred_element_type=F32)
        new = new + old[:, cells].reshape(128, D)
        xo[:, cells] = new.reshape(8, 16, D)
        yo[:, cells] = norm(new, gain_f).astype(BF).reshape(8, 16, D)
    if kind == "outer":
        no[...] = yo[:REACH, :56]
        so[...] = yo[8 - REACH :, :56]


def attend(kind, layer, grid_height, band, q, x, w, e, wout, gf, ga, extra, cost):
    bands = {"inner": (2, 3), "outer": (0, 5), "between": (1, 4)}[kind]

    def rows(a, i):
        return pl.BlockSpec((4,) + a.shape[1:], lambda p: (i, 0, 0))

    banded = (x, x, w, w, e, e)
    queries = () if kind == "inner" else (q, q)
    win = (extra[0],) if kind != "between" else ()
    rest = extra[len(win) :]
    args = (band,) + banded + (wout, gf, ga) + win + queries + rest
    specs = [pl.BlockSpec(memory_space=pltpu.SMEM)] + [rows(a, bands[n % 2]) for n, a in enumerate(banded)]
    specs += [of_layer(wout, layer), whole(gf), whole(ga)] + [of_layer(a, layer) for a in win]
    specs += [rows(a, bands[n % 2]) for n, a in enumerate(queries)] + [whole(a) for a in rest]
    outs = (shape(8, 64, D, dtype=F32), shape(8, 64, D))
    scratch = []
    if kind == "inner":
        outs += (shape(H, 64, D), shape(H, 80, 2 * D))
        scratch += [pltpu.VMEM((H, 80, D), F32)]
    elif kind == "outer":
        outs += (shape(REACH, 56, D), shape(REACH, 56, D), shape(4, 80, 2 * D))
        scratch += [pltpu.VMEM((12, 80, D), F32), pltpu.VMEM((12, 80, 2 * D), BF)]
    scratch += [pltpu.VMEM((2, 64, 512), F32), pltpu.VMEM((8, 64, D), F32)]
    body = functools.partial(attend_kernel, kind, layer, bands, grid_height)
    return call(body, kind, ATTEND_VMEM[kind], 1, args, specs, outs, tuple(whole(o) for o in outs), scratch, cost)


def feed_kernel(layer, last, bands, band_ref, *refs):
    (x_in, x_out, x_mid, y_in, y_out, y_mid, n_ref, s_ref), refs = refs[:8], refs[8:]
    forward_ref, inverse_ref, kernel_ref, expand_ref, shrink_ref, gain_ref = refs[:6]
    outs, (wide, result, spectra) = refs[6:-3], refs[-3:]
    step = pl.program_id(0)

    @pl.when(step == 0)
    def _():
        first = 0
        for piece in (n_ref, y_out[:4], y_mid[:4], y_in, y_mid[4:], y_out[4:], s_ref):
            wide[first : first + piece.shape[0], : piece.shape[1]] = piece[...].astype(F32)
            first += piece.shape[0]

        @pl.when(band_ref[0] == 0)
        def _():
            wide[:REACH] = jnp.zeros((REACH, 64, D), F32)

        @pl.when(band_ref[0] == bands - 1)
        def _():
            wide[REACH + H :] = jnp.zeros((REACH, 64, D), F32)

    count = PAIR * H // PH
    for c in range(PAIR):
        slab = pl.ds(pl.multiple_of((step * PAIR + c) * PW, PW), SLAB)
        for i in range(H // PH):
            x = wide[i * PH : i * PH + LH, slab, :].reshape(LH * SLAB, D).astype(BF)
            first = (c * (H // PH) + i) * 2 * HALF
            t = jnp.dot(forward_ref[...], x, preferred_element_type=F32).astype(BF)
            spectra[first : first + 2 * HALF] = t
    t = spectra[...]

    def expanded(n):
        return jnp.dot(t, expand_ref[:, n * CHUNK : (n + 1) * CHUNK], preferred_element_type=F32)

    def activated(n, z):
        c = slice(n * CHUNK, (n + 1) * CHUNK)
        kr, ki = kernel_ref[:HALF, c], kernel_ref[HALF:, c]
        acts = []
        for i in range(count):
            re, im = z[2 * i * HALF : (2 * i + 1) * HALF], z[(2 * i + 1) * HALF : 2 * (i + 1) * HALF]
            y = jnp.concatenate([(re * kr - im * ki).astype(BF), (re * ki + im * kr).astype(BF)], 0)
            acts.append(gelu(jnp.dot(inverse_ref[...], y, preferred_element_type=F32)).astype(BF))
        return jnp.concatenate(acts, 0)

    def shrunk(n, act):
        return jnp.dot(act, shrink_ref[n * CHUNK : (n + 1) * CHUNK], preferred_element_type=F32)

    acc = jnp.zeros((PAIR * H * PW, D), F32)
    z, act = expanded(0), None
    for n in range(FF // CHUNK):
        ahead = expanded(n + 1) if n + 1 < FF // CHUNK else None
        if act is not None:
            acc = acc + shrunk(n - 1, act)
        act, z = activated(n, z), ahead
    acc = acc + shrunk(FF // CHUNK - 1, act)
    near = pl.ds(pl.multiple_of(step * PAIR * PW, PAIR * PW), PAIR * PW + 8)
    old = [x_out[:4, near], x_mid[:4, near], x_in[:, near], x_mid[4:, near], x_out[4:, near]]
    old = jnp.concatenate(old, 0)
    size = H * PW
    for c in range(PAIR):
        new = acc[c * size : (c + 1) * size].reshape(H, PW, D) + old[:, c * PW + REACH : (c + 1) * PW + REACH]
        result[:, pl.ds(pl.multiple_of((step * PAIR + c) * PW, PW), PW), :] = new

    @pl.when(step == W // PW // PAIR - 1)
    def _():
        if last:
            outs[0][...] = result[...].astype(BF)
            return
        out_ref, on_ref, os_ref, ow_ref, oe_ref = outs
        out_ref[...] = result[...]
        for r in range(H // 6):
            y = norm(result[r * 6 : r * 6 + 6].reshape(6 * W, D), gain_ref[layer + 1 : layer + 2]).astype(BF).reshape(6, W, D)
            if r == 0:
                on_ref[...] = y
            if r == H // 6 - 1:
                os_ref[...] = y
            write_sides(ow_ref, oe_ref, wide, slice(r * 6, r * 6 + 6), y, result[r * 6 : r * 6 + 6])


def feed(last, layer, bands, band, pieces, matrices, kernels, expand, shrink, gain):
    if last:
        outs = (shape(H, W, D),)
    else:
        outs = (shape(H, W, D, dtype=F32),) + edge_shapes()
    args = (band, *pieces, *matrices, kernels, expand, shrink, gain)
    specs = [pl.BlockSpec(memory_space=pltpu.SMEM)]
    specs += [whole(a) for a in (*pieces, *matrices)] + [of_layer(a, layer) for a in (kernels, expand, shrink)]
    return call(
        functools.partial(feed_kernel, layer, last, bands),
        "feed",
        FEED_VMEM,
        W // PW // PAIR,
        args,
        specs + [whole(gain)],
        outs,
        tuple(whole(o) for o in outs),
        [
            pltpu.VMEM((H + 2 * REACH, 64, D), F32),
            pltpu.VMEM((H, W, D), F32),
            pltpu.VMEM((PAIR * H // PH * 2 * HALF, D), BF),
        ],
        24,
    )


def per_device(
    sizes,
    state,
    attention_in,
    attention_out,
    expand_weight,
    depth_kernel,
    shrink_weight,
    norm_attention,
    norm_feedforward,
):
    nlat, nlon = sizes
    north = [(i, (i + 1) % nlat) for i in range(nlat)]
    south = [(b, a) for a, b in north]
    east = [(i, (i + 1) % nlon) for i in range(nlon)]
    west = [(b, a) for a, b in east]

    def trade_lat(n, s):
        return lax.ppermute(s, "lat", north), lax.ppermute(n, "lat", south)

    def trade_lon(w, e):
        return lax.ppermute(e, "lon", east), lax.ppermute(w, "lon", west)

    forward, inverse, taps = transforms()
    matrices = (jnp.asarray(forward, BF), jnp.asarray(inverse, BF))

    band = lax.axis_index("lat").astype(jnp.int32).reshape(1)
    gains_a, gains_f = norm_attention, norm_feedforward
    x = state
    n, s, w, e = first_edges(state, gains_a)
    for layer in range(LAYERS):
        last = layer == LAYERS - 1
        w, e = trade_lon(w, e)
        n, s = trade_lat(n, s)
        qm, kvm = project(layer, x, attention_in, gains_a)
        nc, sc = corners(w, e)
        nc, sc = trade_lat(nc, sc)
        if layer == 0:
            kernels, w, e = lax.optimization_barrier((spectra(taps, depth_kernel), w, e))
        run = functools.partial(attend, layer=layer, grid_height=nlat * H, band=band, wout=attention_out)
        run = functools.partial(run, gf=gains_f, ga=gains_a, x=x, w=w, e=e)
        x_in, y_in, q, kv = run("inner", q=None, extra=(attention_in, qm, kvm, x, w, e), cost=8)
        x_out, y_out, no, so, kvh = run("outer", q=q, extra=(attention_in, kv, n, s, nc, sc), cost=8)
        n, s = trade_lat(no, so)
        x_mid, y_mid = run("between", q=q, extra=(kv, kvh), cost=8)
        x, *edges = feed(
            last,
            layer,
            nlat,
            band,
            (x_in, x_out, x_mid, y_in, y_out, y_mid, n, s),
            matrices,
            kernels,
            expand_weight,
            shrink_weight,
            gains_a,
        )
        if not last:
            n, s, w, e = edges
    return x


def solution(mesh):
    in_specs = (P("lat", "lon", None), P(), P(), P(), P(), P(), P(), P())
    sizes = (mesh.shape["lat"], mesh.shape["lon"])
    return jax.shard_map(
        functools.partial(per_device, sizes),
        mesh=mesh,
        in_specs=in_specs,
        out_specs=P("lat", "lon", None),
        check_vma=False,
    )
```

```python
import functools
import math

import jax
import jax.numpy as jnp
import numpy as np
from jax import lax
from jax.experimental import pallas as pl
from jax.experimental.pallas import tpu as pltpu
from jax.sharding import PartitionSpec as P

BF, F32 = jnp.bfloat16, jnp.float32
D, FF = 512, 2048
RADIUS = 6
REACH = 3
LAYERS = 2
H, W = 24, 48
PH, PW = 12, 8
LH, LW = PH + 2 * REACH, PW + 2 * REACH
SLAB = 16
SIDE = RADIUS + REACH
HALF = LH * LW // 2 + 2
CHUNK = 256
PAIR = 2
PROJECT_VMEM, FEED_VMEM = 12, 20
ATTEND_VMEM = {"inner": 18, "outer": 14, "between": 10}


def transforms():
    seen, reps = set(), []
    for a in range(LH):
        for b in range(LW):
            mirror = ((-a) % LH, (-b) % LW)
            if mirror not in seen:
                seen.add((a, b))
                reps.append((a / LH, b / LW, (1.0 if mirror == (a, b) else 2.0) / (LH * LW)))
    fa, fb, weight = np.array(reps).T[:, :, None, None]
    angle = 2 * np.pi * (fa * np.arange(LH)[:, None] + fb * np.arange(LW))
    cos, sin = np.cos(angle), np.sin(angle)
    sin[np.abs(sin) < 1e-9] = 0
    forward = np.zeros((2 * HALF, LH, SLAB))
    forward[:HALF, :, :LW] = cos
    forward[HALF:, :, :LW] = -sin
    inverse = np.concatenate(
        [cos[:, :PH, :PW].reshape(HALF, -1).T, -sin[:, :PH, :PW].reshape(HALF, -1).T], 1
    )
    taps = np.concatenate([(cos * weight)[:, :7, :7], (sin * weight)[:, :7, :7]], 0)
    return forward.reshape(2 * HALF, -1), inverse, taps.reshape(2 * HALF, -1)


def norm(x, gain):
    c = x - jnp.mean(x, axis=-1, keepdims=True)
    return c * lax.rsqrt(jnp.mean(c * c, axis=-1, keepdims=True) + 1e-5) * gain


def gelu(x):
    return 0.5 * x * (1.0 + lax.erf(x * np.float32(1 / math.sqrt(2))))


def whole(a):
    return pl.BlockSpec(a.shape, lambda p: (0,) * len(a.shape))


def of_layer(a, layer):
    return pl.BlockSpec((None,) + a.shape[1:], lambda p: (layer,) + (0,) * (len(a.shape) - 1))


def shape(*dims, dtype=BF):
    return jax.ShapeDtypeStruct(dims, dtype)


def call(body, name, limit, grid, args, specs, outs, out_specs, scratch, cost):
    return pl.pallas_call(
        body,
        grid=(grid,),
        in_specs=specs,
        out_specs=out_specs,
        out_shape=outs,
        scratch_shapes=scratch,
        compiler_params=pltpu.CompilerParams(vmem_limit_bytes=limit * 2**20),
        cost_estimate=pl.CostEstimate(flops=int(cost * 6e8), bytes_accessed=10**6, transcendentals=0),
        name=name,
    )(*args)


def write_sides(ow_ref, oe_ref, room, rows, normed, stream):
    for ref, near, inner, outer in (
        (ow_ref, slice(0, 16), slice(0, SIDE), slice(0, REACH)),
        (oe_ref, slice(W - 16, W), slice(16 - SIDE, 16), slice(16 - REACH, 16)),
    ):
        room[:6, :SIDE] = normed.astype(F32)[:, near][:, inner]
        room[:6, SIDE : SIDE + REACH] = stream[:, near][:, outer]
        ref[rows] = room[:6, : SIDE + REACH].astype(BF)


def edge_shapes():
    rows, cols = shape(RADIUS, W, D), shape(H, SIDE + REACH, D)
    return (rows, rows, cols, cols)


def edges_kernel(x_ref, gain_ref, on_ref, os_ref, ow_ref, oe_ref, room):
    for r in range(0, H, 6):
        x = x_ref[r : r + 6].astype(F32)
        y = norm(x, gain_ref[:1]).astype(BF)
        if r == 0:
            on_ref[...] = y
        if r == H - 6:
            os_ref[...] = y
        write_sides(ow_ref, oe_ref, room, slice(r, r + 6), y, x)


def first_edges(x, gains):
    outs = edge_shapes()
    room = [pltpu.VMEM((6, 16, D), F32)]
    specs, out_specs = [whole(x), whole(gains)], tuple(whole(o) for o in outs)
    return call(edges_kernel, "edges", PROJECT_VMEM, 1, (x, gains), specs, outs, out_specs, room, 1)


def spectra_kernel(taps_ref, kernel_ref, out_ref, room):
    for layer in range(LAYERS):
        for a in range(7):
            room[7 * a : 7 * a + 7] = kernel_ref[layer, a].astype(F32)
        room[49:] = jnp.zeros((7, FF), F32)
        for n in range(0, FF, 512):
            c = slice(n, n + 512)
            got = jnp.dot(taps_ref[...], room[:, c], precision=lax.Precision.HIGHEST, preferred_element_type=F32)
            out_ref[layer, :, c] = got.astype(BF)


def spectra(taps, depth_kernel):
    outs = shape(LAYERS, 2 * HALF, FF)
    taps = jnp.asarray(np.pad(taps, ((0, 0), (0, 7))), F32)
    args = (taps, depth_kernel)
    specs = [whole(a) for a in args]
    return call(spectra_kernel, "spectra", 16, 1, args, specs, outs, whole(outs), [pltpu.VMEM((56, FF), F32)], 1)


def corners_kernel(wn, en, ws, es, nc_ref, sc_ref, room):
    for west, east, ref in ((wn, en, nc_ref), (ws, es, sc_ref)):
        room[:, : SIDE + REACH] = west[...].astype(F32)
        room[:, SIDE + REACH : 2 * (SIDE + REACH)] = east[...].astype(F32)
        ref[...] = room[...].astype(BF)


def corners(w, e):
    def rows(i):
        return pl.BlockSpec((RADIUS,) + w.shape[1:], lambda p: (i, 0, 0))

    last = H // RADIUS - 1
    outs = (shape(RADIUS, 2 * (SIDE + REACH), D),) * 2
    specs, out_specs = [rows(0), rows(0), rows(last), rows(last)], tuple(whole(o) for o in outs)
    room = [pltpu.VMEM((RADIUS, 2 * (SIDE + REACH), D), F32)]
    return call(corners_kernel, "corners", 4, 1, (w, e, w, e), specs, outs, out_specs, room, 0.1)


def scaled(q):
    return (q * np.float32(0.125 / math.log(2))).astype(BF)


def project_kernel(layer, x_ref, win_ref, gain_ref, q_ref, kv_ref):
    gain = gain_ref[layer : layer + 1]
    for r in range(0, H, 6):
        rows = slice(r, r + 6)
        y = norm(x_ref[rows].astype(F32).reshape(6 * W, D), gain).reshape(6, W, D)
        q = y[:, 16 - REACH : 48 - REACH].reshape(6 * 32, D).astype(BF)
        q_ref[rows] = scaled(jnp.dot(q, win_ref[:, :D], preferred_element_type=F32)).reshape(6, 32, D)
        y = y[:, 16 - SIDE : 48 - SIDE].reshape(6 * 32, D).astype(BF)
        kv_ref[rows] = jnp.dot(y, win_ref[:, D:], preferred_element_type=F32).astype(BF).reshape(6, 32, 2 * D)


def project(layer, x, win, gains):
    outs = (shape(H, 32, D), shape(H, 32, 2 * D))
    specs = [whole(x), of_layer(win, layer), whole(gains)]
    body = functools.partial(project_kernel, layer)
    return call(body, "project", PROJECT_VMEM, 1, (x, win, gains), specs, outs, tuple(whole(o) for o in outs), [], 0.2)


def fill_mask(mask, t, i, band, grid_height):
    row = lax.broadcasted_iota(jnp.int32, (64, 512), 0)
    col = lax.broadcasted_iota(jnp.int32, (64, 512), 1)
    a, b, u, v = row >> 4, row & 15, col >> 5, col & 31
    lat = band * H + i * 4 - RADIUS + u
    ok = (u >= a) & (u <= a + 12) & (v >= b) & (v <= b + 12) & (lat >= 0) & (lat < grid_height)
    mask[t] = jnp.where(ok, 0.0, -jnp.inf)


def scores(q, k, mask):
    head = lax.broadcasted_iota(jnp.int32, (64, 256), 1) >> 6
    apart = jnp.concatenate([jnp.where(head == h, q, jnp.zeros_like(q)) for h in range(4)], 0)
    s = lax.dot_general(apart, k, (((1,), (1,)), ((), ())), preferred_element_type=F32)
    return (s.reshape(4, 64, 512) + mask[None]).reshape(256, 512)


def weighted(s, v):
    head = lax.broadcasted_iota(jnp.int32, (64, 256), 1) >> 6
    p = jnp.exp2(s - jnp.max(s, axis=1, keepdims=True))
    total = jnp.sum(p, axis=1, keepdims=True)
    o = jnp.dot(p.astype(BF), v, preferred_element_type=F32) * (1.0 / total)
    r = o[192:]
    for h in range(3):
        r = jnp.where(head == h, o[h * 64 : (h + 1) * 64], r)
    return r.astype(BF)


def attend_blocks(blocks):
    groups = [
        (qb[:, c], pairs[:, c], pairs[:, D + c.start : D + c.stop], mask)
        for qb, pairs, mask in blocks
        for c in (slice(0, 256), slice(256, 512))
    ]
    ahead, outs = scores(groups[0][0], groups[0][1], groups[0][3]), []
    for n, (_, _, v, _) in enumerate(groups):
        now = ahead
        if n + 1 < len(groups):
            q, k, _, mask = groups[n + 1]
            ahead = scores(q, k, mask)
        outs.append(weighted(now, v))
    return [jnp.concatenate(outs[n : n + 2], 1) for n in range(0, len(outs), 2)]


def attend_kernel(kind, layer, bands, grid_height, band_ref, *refs):
    (x0, x1, w0, w1, e0, e1, wout_ref, gf_ref, ga), refs = refs[:9], refs[9:]
    gain_a, gain_f = ga[layer : layer + 1], gf_ref[layer : layer + 1]

    def project_pairs(y, win):
        return jnp.dot(y.astype(BF), win[:, D:], preferred_element_type=F32).astype(BF)

    refs, (masks, old) = refs[:-2], refs[-2:]
    for t in range(2):
        fill_mask(masks, t, bands[t], band_ref[0], grid_height)
        rows = slice(4 * t, 4 * t + 4)
        west, east = (w0, w1)[t][...].astype(F32), (e0, e1)[t][...].astype(F32)
        old[rows, :REACH] = west[:, SIDE:]
        old[rows, REACH : REACH + W] = (x0, x1)[t][...].astype(F32)
        old[rows, REACH + W : W + 2 * REACH] = east[:, SIDE:]
        old[rows, W + 2 * REACH :] = jnp.zeros((4, 64 - W - 2 * REACH, D), F32)
    if kind == "inner":
        win, qm, kvm, x, w, e, xo, yo, q, kv, wide = refs
        west = w[...].astype(F32)[:, :SIDE]
        east = e[...].astype(F32)[:, :SIDE]
        left = norm(x[:, :16].astype(F32), gain_a)
        right = norm(x[:, 32:].astype(F32), gain_a)
        wide[:, :SIDE] = west
        wide[:, SIDE:16] = left[:, : 16 - SIDE]
        wide[:, 16:25] = right[:, 16 - SIDE :]
        wide[:, 25 : 25 + SIDE] = east
        wide[:, 25 + SIDE : 48] = jnp.zeros((H, 23 - SIDE, D), F32)
        wide[:, 48 : 48 + REACH] = west[:, RADIUS:]
        wide[:, 48 + REACH : 64] = left[:, : 16 - REACH]
        wide[:, 64 : 64 + REACH] = right[:, 16 - REACH :]
        wide[:, 64 + REACH : 64 + 2 * REACH] = east[:, :REACH]
        wide[:, 64 + 2 * REACH :] = jnp.zeros((H, 16 - 2 * REACH, D), F32)
        for r in range(0, H, 12):
            rows = slice(r, r + 12)
            y = project_pairs(wide[rows, :48].reshape(12 * 48, D), win).reshape(12, 48, 2 * D)
            kv[rows, :16] = y[:, :16]
            kv[rows, 48:] = y[:, 16:]
            y = wide[rows, 48:].reshape(12 * 32, D).astype(BF)
            y = scaled(jnp.dot(y, win[:, :D], preferred_element_type=F32)).reshape(12, 32, D)
            q[rows, :16] = y[:, :16]
            q[rows, 48:] = y[:, 16:]
        kv[:, 16:48] = kvm[...]
        q[:, 16:48] = qm[...]
        qs = [q[4 * i : 4 * i + 4] for i in bands]

        def window(t, c):
            return kv[bands[t] * 4 - RADIUS : bands[t] * 4 - RADIUS + 16, c]

    elif kind == "outer":
        win, q0, q1, kv, n, s, nc, sc, xo, yo, no, so, kvh, wide, halo = refs
        qs = [q0, q1]
        wide[:, 2 * SIDE + W :] = jnp.zeros((12, 80 - 2 * SIDE - W, D), F32)
        for first, middle, corners in ((0, n, nc), (6, s, sc)):
            rows = slice(first, first + 6)
            sides = corners[...].astype(F32)
            wide[rows, :SIDE] = sides[:, :SIDE]
            wide[rows, SIDE : SIDE + W] = middle[...].astype(F32)
            wide[rows, SIDE + W : 2 * SIDE + W] = sides[:, SIDE + REACH : 2 * SIDE + REACH]
        halo[...] = project_pairs(wide[...].reshape(12 * 80, D), win).reshape(12, 80, 2 * D)
        kvh[...] = halo[4:8]

        def window(t, c):
            parts = (kv[14:, c], halo[6:, c]) if t else (halo[:6, c], kv[:10, c])
            return jnp.concatenate(parts, 0)

    else:
        q0, q1, kv, kvh, xo, yo = refs
        qs = [q0, q1]

        def window(t, c):
            parts = (kv[10:, c], kvh[2:, c]) if t else (kvh[:2, c], kv[:14, c])
            return jnp.concatenate(parts, 0)

    blocks = []
    for j in range(4):
        for t in range(2):
            pairs = window(t, slice(j * 16, j * 16 + 32)).reshape(512, 2 * D)
            blocks.append((qs[t][:, j * 16 : j * 16 + 16].reshape(64, D), pairs, masks[t]))
    mixed = attend_blocks(blocks)
    for j in range(4):
        cells = slice(j * 16, j * 16 + 16)
        new = jnp.dot(jnp.concatenate(mixed[2 * j : 2 * j + 2], 0), wout_ref[...], preferred_element_type=F32)
        new = new + old[:, cells].reshape(128, D)
        xo[:, cells] = new.reshape(8, 16, D)
        yo[:, cells] = norm(new, gain_f).astype(BF).reshape(8, 16, D)
    if kind == "outer":
        no[...] = yo[:REACH, :56]
        so[...] = yo[8 - REACH :, :56]


def attend(kind, layer, grid_height, band, q, x, w, e, wout, gf, ga, extra, cost):
    bands = {"inner": (2, 3), "outer": (0, 5), "between": (1, 4)}[kind]

    def rows(a, i):
        return pl.BlockSpec((4,) + a.shape[1:], lambda p: (i, 0, 0))

    banded = (x, x, w, w, e, e)
    queries = () if kind == "inner" else (q, q)
    win = (extra[0],) if kind != "between" else ()
    rest = extra[len(win) :]
    args = (band,) + banded + (wout, gf, ga) + win + queries + rest
    specs = [pl.BlockSpec(memory_space=pltpu.SMEM)] + [rows(a, bands[n % 2]) for n, a in enumerate(banded)]
    specs += [of_layer(wout, layer), whole(gf), whole(ga)] + [of_layer(a, layer) for a in win]
    specs += [rows(a, bands[n % 2]) for n, a in enumerate(queries)] + [whole(a) for a in rest]
    outs = (shape(8, 64, D, dtype=F32), shape(8, 64, D))
    scratch = []
    if kind == "inner":
        outs += (shape(H, 64, D), shape(H, 80, 2 * D))
        scratch += [pltpu.VMEM((H, 80, D), F32)]
    elif kind == "outer":
        outs += (shape(REACH, 56, D), shape(REACH, 56, D), shape(4, 80, 2 * D))
        scratch += [pltpu.VMEM((12, 80, D), F32), pltpu.VMEM((12, 80, 2 * D), BF)]
    scratch += [pltpu.VMEM((2, 64, 512), F32), pltpu.VMEM((8, 64, D), F32)]
    body = functools.partial(attend_kernel, kind, layer, bands, grid_height)
    return call(body, kind, ATTEND_VMEM[kind], 1, args, specs, outs, tuple(whole(o) for o in outs), scratch, cost)


def feed_kernel(layer, last, bands, band_ref, *refs):
    (x_in, x_out, x_mid, y_in, y_out, y_mid, n_ref, s_ref), refs = refs[:8], refs[8:]
    forward_ref, inverse_ref, kernel_ref, expand_ref, shrink_ref, gain_ref = refs[:6]
    outs, (wide, result, spectra) = refs[6:-3], refs[-3:]
    step = pl.program_id(0)

    @pl.when(step == 0)
    def _():
        first = 0
        for piece in (n_ref, y_out[:4], y_mid[:4], y_in, y_mid[4:], y_out[4:], s_ref):
            wide[first : first + piece.shape[0], : piece.shape[1]] = piece[...].astype(F32)
            first += piece.shape[0]

        @pl.when(band_ref[0] == 0)
        def _():
            wide[:REACH] = jnp.zeros((REACH, 64, D), F32)

        @pl.when(band_ref[0] == bands - 1)
        def _():
            wide[REACH + H :] = jnp.zeros((REACH, 64, D), F32)

    count = PAIR * H // PH
    for c in range(PAIR):
        slab = pl.ds(pl.multiple_of((step * PAIR + c) * PW, PW), SLAB)
        for i in range(H // PH):
            x = wide[i * PH : i * PH + LH, slab, :].reshape(LH * SLAB, D).astype(BF)
            first = (c * (H // PH) + i) * 2 * HALF
            t = jnp.dot(forward_ref[...], x, preferred_element_type=F32).astype(BF)
            spectra[first : first + 2 * HALF] = t
    t = spectra[...]

    def expanded(n):
        return jnp.dot(t, expand_ref[:, n * CHUNK : (n + 1) * CHUNK], preferred_element_type=F32)

    def activated(n, z):
        c = slice(n * CHUNK, (n + 1) * CHUNK)
        kr, ki = kernel_ref[:HALF, c], kernel_ref[HALF:, c]
        acts = []
        for i in range(count):
            re = z[2 * i * HALF : (2 * i + 1) * HALF].astype(BF)
            im = z[(2 * i + 1) * HALF : 2 * (i + 1) * HALF].astype(BF)
            y = jnp.concatenate([re * kr - im * ki, re * ki + im * kr], 0)
            acts.append(gelu(jnp.dot(inverse_ref[...], y, preferred_element_type=F32)).astype(BF))
        return jnp.concatenate(acts, 0)

    def shrunk(n, act):
        return jnp.dot(act, shrink_ref[n * CHUNK : (n + 1) * CHUNK], preferred_element_type=F32)

    acc = jnp.zeros((PAIR * H * PW, D), F32)
    z, act = expanded(0), None
    for n in range(FF // CHUNK):
        ahead = expanded(n + 1) if n + 1 < FF // CHUNK else None
        if act is not None:
            acc = acc + shrunk(n - 1, act)
        act, z = activated(n, z), ahead
    acc = acc + shrunk(FF // CHUNK - 1, act)
    near = pl.ds(pl.multiple_of(step * PAIR * PW, PAIR * PW), PAIR * PW + 8)
    old = [x_out[:4, near], x_mid[:4, near], x_in[:, near], x_mid[4:, near], x_out[4:, near]]
    old = jnp.concatenate(old, 0)
    size = H * PW
    for c in range(PAIR):
        new = acc[c * size : (c + 1) * size].reshape(H, PW, D) + old[:, c * PW + REACH : (c + 1) * PW + REACH]
        result[:, pl.ds(pl.multiple_of((step * PAIR + c) * PW, PW), PW), :] = new

    @pl.when(step == W // PW // PAIR - 1)
    def _():
        if last:
            outs[0][...] = result[...].astype(BF)
            return
        out_ref, on_ref, os_ref, ow_ref, oe_ref = outs
        out_ref[...] = result[...]
        for r in range(H // 6):
            y = norm(result[r * 6 : r * 6 + 6].reshape(6 * W, D), gain_ref[layer + 1 : layer + 2]).astype(BF).reshape(6, W, D)
            if r == 0:
                on_ref[...] = y
            if r == H // 6 - 1:
                os_ref[...] = y
            write_sides(ow_ref, oe_ref, wide, slice(r * 6, r * 6 + 6), y, result[r * 6 : r * 6 + 6])


def feed(last, layer, bands, band, pieces, matrices, kernels, expand, shrink, gain):
    if last:
        outs = (shape(H, W, D),)
    else:
        outs = (shape(H, W, D, dtype=F32),) + edge_shapes()
    args = (band, *pieces, *matrices, kernels, expand, shrink, gain)
    specs = [pl.BlockSpec(memory_space=pltpu.SMEM)]
    specs += [whole(a) for a in (*pieces, *matrices)] + [of_layer(a, layer) for a in (kernels, expand, shrink)]
    return call(
        functools.partial(feed_kernel, layer, last, bands),
        "feed",
        FEED_VMEM,
        W // PW // PAIR,
        args,
        specs + [whole(gain)],
        outs,
        tuple(whole(o) for o in outs),
        [
            pltpu.VMEM((H + 2 * REACH, 64, D), F32),
            pltpu.VMEM((H, W, D), F32),
            pltpu.VMEM((PAIR * H // PH * 2 * HALF, D), BF),
        ],
        24,
    )


def per_device(
    sizes,
    state,
    attention_in,
    attention_out,
    expand_weight,
    depth_kernel,
    shrink_weight,
    norm_attention,
    norm_feedforward,
):
    nlat, nlon = sizes
    north = [(i, (i + 1) % nlat) for i in range(nlat)]
    south = [(b, a) for a, b in north]
    east = [(i, (i + 1) % nlon) for i in range(nlon)]
    west = [(b, a) for a, b in east]

    def trade_lat(n, s):
        return lax.ppermute(s, "lat", north), lax.ppermute(n, "lat", south)

    def trade_lon(w, e):
        return lax.ppermute(e, "lon", east), lax.ppermute(w, "lon", west)

    forward, inverse, taps = transforms()
    matrices = (jnp.asarray(forward, BF), jnp.asarray(inverse, BF))

    band = lax.axis_index("lat").astype(jnp.int32).reshape(1)
    gains_a, gains_f = norm_attention, norm_feedforward
    x = state
    n, s, w, e = first_edges(state, gains_a)
    for layer in range(LAYERS):
        last = layer == LAYERS - 1
        w, e = trade_lon(w, e)
        n, s = trade_lat(n, s)
        qm, kvm = project(layer, x, attention_in, gains_a)
        nc, sc = corners(w, e)
        nc, sc = trade_lat(nc, sc)
        if layer == 0:
            kernels, w, e = lax.optimization_barrier((spectra(taps, depth_kernel), w, e))
        run = functools.partial(attend, layer=layer, grid_height=nlat * H, band=band, wout=attention_out)
        run = functools.partial(run, gf=gains_f, ga=gains_a, x=x, w=w, e=e)
        x_in, y_in, q, kv = run("inner", q=None, extra=(attention_in, qm, kvm, x, w, e), cost=8)
        x_out, y_out, no, so, kvh = run("outer", q=q, extra=(attention_in, kv, n, s, nc, sc), cost=8)
        n, s = trade_lat(no, so)
        x_mid, y_mid = run("between", q=q, extra=(kv, kvh), cost=8)
        x, *edges = feed(
            last,
            layer,
            nlat,
            band,
            (x_in, x_out, x_mid, y_in, y_out, y_mid, n, s),
            matrices,
            kernels,
            expand_weight,
            shrink_weight,
            gains_a,
        )
        if not last:
            n, s, w, e = edges
    return x


def solution(mesh):
    in_specs = (P("lat", "lon", None), P(), P(), P(), P(), P(), P(), P())
    sizes = (mesh.shape["lat"], mesh.shape["lon"])
    return jax.shard_map(
        functools.partial(per_device, sizes),
        mesh=mesh,
        in_specs=in_specs,
        out_specs=P("lat", "lon", None),
        check_vma=False,
    )
```
